512 devices in a mesh: lat: 8 (over x, core), rad: 64 (over z, y).
Axes of the slice: x: 4, y: 8, z: 8, core: 2. Of those that a mesh axis runs over, the one named last changes fastest.
Arguments:
- forcing: bfloat16 [512, 768, 1024], P('rad', 'lat'), may hold values from -6 to 6
- legendre: bfloat16 [256, 512, 768], P('rad', None, 'lat'), may hold values from -0.3125 to 0.3125
- assign: int32 [256], replicated, may hold values from 0 to 511, as said below
- inverse: float32 [512, 512, 512], P(('lat', 'rad')), may hold values from -0.25 to 0.25
- previous: bfloat16 [512, 512, 512], P('rad', 'lat'), may hold values from -6 to 6
Outputs:
- new_state: bfloat16 [512, 512, 512], P('rad', 'lat')
The draws below stay inside these ranges and needn't reach their ends.
Inputs may be any that keep to these rules, and one draw needn't show every extreme that they name: `assign`: the 256 orders are distinct; 0 and 511 are among them.
All inputs are finite; a program needn't handle non-finite values.
Results may differ from the reference program's by a relative error of at most 0.01.
Values may be sent and summed in bfloat16 or wider, within the bound.
No kernel may reach another device: no remote copies, remote signals or barrier semaphores. Data moves between devices by JAX's collectives and lax.ppermute only.
A program may use at most 64 MiB of HBM per device.

```python
import math
import jax
import jax.numpy as jnp
from jax import lax

NR = 512
L = 512
NLAT = 768
NLON = 1024
NMW = 256
N_LAT = 8


def draw_assign(key, part):
    key = jax.random.fold_in(key, 7)
    inner_orders = jax.random.permutation(key, L - 2)[:NMW - 2] + 1
    chosen_orders = jnp.concatenate([jnp.array([0, L - 1], jnp.int32), inner_orders.astype(jnp.int32)])
    return jax.random.permutation(jax.random.fold_in(key, 1), chosen_orders).astype(jnp.int32)


def with_spikes(drawn, rng, source, target, blocks, factor):
    def block_of(axis_at):
        return (jnp.arange(drawn.shape[axis_at]) // (drawn.shape[axis_at] // blocks)).reshape((-1,) + (1,) * (drawn.ndim - 1 - axis_at))

    one_side = jax.random.permutation(rng, blocks)[block_of(target)]
    other_side = (block_of(target) + blocks // 2) % blocks
    return jnp.where((block_of(source) == one_side) | (block_of(source) == other_side), factor * drawn, drawn)


def block_scale(rng, extent, cuts, low, top_value):
    def one(position, parts):
        draws = jax.random.uniform(jax.random.fold_in(jax.random.fold_in(rng, 6), position), (parts,), jnp.float32, low / len(cuts), top_value / len(cuts))
        return jnp.repeat(jnp.exp(draws), extent[position] // parts).reshape((-1,) + (1,) * (len(extent) - position - 1))

    gain = one(*cuts[0])
    for cut in cuts[1:]:
        gain = gain * one(*cut)
    return gain


def noise(stream_key, extent, deviation, limit, cuts=(), held_as=jnp.bfloat16):
    loudness = block_scale(stream_key, extent, cuts, -0.22, 0.18) if cuts else 1.0
    result = jax.random.normal(stream_key, extent, jnp.float32) * deviation * loudness
    return jnp.minimum(jnp.maximum(result, -limit), limit).astype(held_as)


def gaussian_with(rng, shape, spread, reach, shards, heavy, kind=jnp.bfloat16):
    values = spread * jax.random.normal(rng, shape, jnp.float32)
    if shards:
        values = values * block_scale(rng, shape, shards, -0.22, 0.18)
    return jnp.clip(with_spikes(values, jax.random.fold_in(rng, 3), *heavy), -reach, reach).astype(kind)


def setup_inputs(seed: int = 0) -> dict:
    streams_of = jax.random.split(jax.random.key(seed), 6)
    return {
        "forcing": noise(streams_of[0], (NR, NLAT, NLON), 1.0, 6.0, ((0, 64), (1, 8))),
        "legendre": gaussian_with(streams_of[1], (NMW, L, NLAT), NLAT ** -0.5, 0.3125, ((0, 64), (2, 8)), (2, 1, 8, 2.0)),
        "assign": draw_assign(jax.random.fold_in(streams_of[5], 71), 0),
        "inverse": noise(streams_of[3], (L, NR, NR), NR ** -0.5, 0.25, ((0, 512),), jnp.float32),
        "previous": noise(streams_of[4], (NR, L, 2 * NMW), 1.0, 6.0, ((0, 64), (1, 8))),
    }


time_step = 0.5

def fourier_table(assign, lon_count):
    longitude = jnp.arange(lon_count, dtype=jnp.int32)
    phases = assign[:, None] * longitude[None, :] % lon_count
    angles = phases.astype(jnp.float32) * (2.0 * math.pi / lon_count)
    norm_scale = 1.0 / math.sqrt(lon_count)
    stacked = jnp.stack([jnp.cos(angles), -jnp.sin(angles)], axis=1) * norm_scale
    return stacked.reshape(2 * assign.shape[0], lon_count).T.astype(jnp.bfloat16)

def reference(forcing, legendre, assign, inverse, previous):
    table_values = fourier_table(assign, NLON)
    fourier = jnp.dot(forcing.reshape(NR * NLAT, NLON), table_values, preferred_element_type=jnp.float32)
    fourier = fourier.astype(jnp.bfloat16).reshape(NR, NLAT, NMW, 2)
    ell_index = jnp.arange(L, dtype=jnp.int32)
    keep_mask = (ell_index[None, :, None] >= assign[:, None, None]).astype(jnp.bfloat16)
    masked = legendre * keep_mask
    block_rows = NLAT // N_LAT

    def add_block(summed, block_index):
        first_row = (block_index * block_rows).astype(jnp.int32)
        leg_block = lax.dynamic_slice_in_dim(masked, first_row, block_rows, 2).astype(jnp.float32)
        grid_part = lax.dynamic_slice_in_dim(fourier, first_row, block_rows, 1).astype(jnp.float32)
        partial_sum = jnp.einsum('kel,rlkc->ekcr', leg_block, grid_part)
        rounded = lax.optimization_barrier(partial_sum.astype(jnp.bfloat16))
        return (summed + rounded.astype(jnp.float32), None)
    initial = jnp.zeros((L, NMW, 2, NR), jnp.float32)
    spectrum, unused = lax.scan(add_block, initial, jnp.arange(N_LAT, dtype=jnp.int32))
    prior_modes = previous.astype(jnp.float32).reshape(NR, L, NMW, 2).transpose(1, 2, 3, 0)
    right_side = prior_modes + time_step * spectrum
    solved = jnp.einsum('ekcr,esr->ekcs', right_side, inverse, precision=lax.Precision.HIGHEST)
    valid_mask = (assign[None, :] <= ell_index[:, None]).astype(jnp.float32)
    solved = solved * valid_mask[:, :, None, None]
    return solved.astype(jnp.bfloat16).transpose(3, 0, 1, 2).reshape(NR, L, 2 * NMW)
```

```python
import math

import jax
import jax.numpy as jnp
from jax import lax
from jax.experimental import pallas as pl
from jax.experimental.pallas import tpu as pltpu
from jax.sharding import Mesh, PartitionSpec as P

NR = 512
L = 512
LON = 1024
BF = jnp.bfloat16
F32 = jnp.float32
RAD = ("z", "y")
LAT = ("x", "core")


def nt_dot(a, b):
    return lax.dot_general(a, b, (((1,), (1,)), ((), ())), preferred_element_type=F32)


def iota(shape, dim):
    return lax.broadcasted_iota(jnp.int32, shape, dim)


def regroup():
    row, column = iota((512, 512), 0), iota((512, 512), 1)
    return column == (row & 63) * 8 + (row >> 6)


def cos_sin(phase):
    quadrant = ((phase + 128) >> 8) & 3
    rest = ((phase + 128) & 255) - 128
    x = rest.astype(F32) * (2.0 * math.pi / LON)
    x2 = x * x
    sin_x = x * (1.0 + x2 * (-1.0 / 6 + x2 * (1.0 / 120 + x2 * (-1.0 / 5040 + x2 * (1.0 / 362880)))))
    cos_x = 1.0 + x2 * (-0.5 + x2 * (1.0 / 24 + x2 * (-1.0 / 720 + x2 * (1.0 / 40320))))
    swap = (quadrant & 1) == 1
    cos_part = jnp.where(swap, sin_x, cos_x)
    sin_part = jnp.where(swap, cos_x, sin_x)
    cos_sign = jnp.where((quadrant == 1) | (quadrant == 2), -1.0, 1.0)
    sin_sign = jnp.where(quadrant >= 2, -1.0, 1.0)
    return cos_part * cos_sign, sin_part * sin_sign


def fourier_kernel(assign_ref, forcing_ref, previous_ref, out_ref, table_ref):
    row, lane = iota((256, 256), 0), iota((256, 256), 1)
    mine = lane == (row & 63) * 4 + (row >> 6)
    orders = jnp.sum(jnp.where(mine, assign_ref[...], 0), axis=1, keepdims=True)
    lane = iota((256, 128), 1)
    cos_low, sin_low = cos_sin((orders * lane) & (LON - 1))
    cos_high, sin_high = cos_sin((orders * 128 * lane) & (LON - 1))
    scale = LON**-0.5
    cos_low, sin_low = cos_low * scale, sin_low * scale
    for q in range(LON // 128):
        ch, sh = cos_high[:, q : q + 1], sin_high[:, q : q + 1]
        real = (cos_low * ch - sin_low * sh).astype(BF)
        imag = (-(sin_low * ch + cos_low * sh)).astype(BF)
        for x in range(4):
            table_ref[x * 128 : x * 128 + 64, q * 128 : q * 128 + 128] = real[x * 64 : x * 64 + 64]
            table_ref[x * 128 + 64 : x * 128 + 128, q * 128 : q * 128 + 128] = imag[x * 64 : x * 64 + 64]
    table = table_ref[...]
    for h in range(3):
        part = forcing_ref[:, h * 32 : h * 32 + 32, :].reshape(256, LON)
        out_ref[:, h * 256 : h * 256 + 256] = nt_dot(table, part).astype(BF)
    out_ref[:, 768:1280] = nt_dot(regroup().astype(BF), previous_ref[...].reshape(512, 512)).astype(BF)


def legendre_kernel(assign_ref, place_ref, legendre_ref, out_ref):
    slot = place_ref[0]
    lane = iota((1, 256), 1)
    order = jnp.sum(jnp.where(lane == slot, assign_ref[...], 0), axis=1, keepdims=True)
    row, column = iota((512, 512), 0), iota((512, 512), 1)
    degree = (row & 7) * 64 + (row >> 3)
    pick = column == degree
    kept = jnp.where(pick & (degree >= order), 1.0, 0.0).astype(BF)
    for h in range(3):
        for quad in range(2):
            pieces = []
            for i in range(4):
                g = quad * 4 + i
                pieces.append(legendre_ref[g % 2, g // 2, h * 32 : h * 32 + 32, :])
            at = h * 256 + quad * 128
            out_ref[:, at : at + 128] = nt_dot(kept, jnp.concatenate(pieces, axis=0)).astype(BF)
    out_ref[:, 768:1280] = jnp.where(pick, 2.0, 0.0).astype(BF)


def roll(a, shift):
    return pltpu.roll(a, shift, 1)


def spectrum_kernel(arrived_ref, weights_ref, out_ref, gathered_ref):
    lane = iota((64, 128), 1)
    low_half = lane < 64
    even_quarter = (lane & 32) == 0

    def tile(g, at):
        return arrived_ref[g * 64 : g * 64 + 64, at : at + 128].astype(F32)

    def place(rho, at, value):
        gathered_ref[rho * 64 : rho * 64 + 64, at : at + 128] = value.astype(BF)

    for h in range(3):
        for high in range(2):
            for quad in range(2):
                a = [tile(quad * 4 + i, h * 256 + high * 128) for i in range(4)]
                b0 = jnp.where(low_half, a[0], roll(a[2], 64))
                b2 = jnp.where(low_half, roll(a[0], 64), a[2])
                b1 = jnp.where(low_half, a[1], roll(a[3], 64))
                b3 = jnp.where(low_half, roll(a[1], 64), a[3])
                c = [
                    jnp.where(even_quarter, b0, roll(b1, 32)),
                    jnp.where(even_quarter, roll(b0, 96), b1),
                    jnp.where(even_quarter, b2, roll(b3, 32)),
                    jnp.where(even_quarter, roll(b2, 96), b3),
                ]
                for i in range(4):
                    place(high * 4 + i, h * 256 + quad * 128, c[i])
    for pair in range(4):
        for two in range(4):
            at = 768 + pair * 128
            a0, a1 = tile(two * 2, at), tile(two * 2 + 1, at)
            to = 768 + two * 128
            place(pair * 2, to, jnp.where(low_half, a0, roll(a1, 64)))
            place(pair * 2 + 1, to, jnp.where(low_half, roll(a0, 64), a1))
    out_ref[...] = nt_dot(weights_ref[...], gathered_ref[...]).astype(BF)


def inverse_kernel(assign_ref, place_ref, inverse_ref, out_ref, valid_ref):
    out_ref[...] = nt_dot(inverse_ref[0].astype(BF), regroup().astype(BF)).astype(BF)
    valid = jnp.where(assign_ref[...] <= place_ref[1], 1.0, 0.0)
    row, column = iota((256, 512), 0), iota((256, 512), 1)
    doubled = (row == (column >> 1)).astype(BF)
    valid_ref[...] = jnp.dot(
        jnp.broadcast_to(valid, (8, 256)).astype(BF), doubled, preferred_element_type=F32
    )


def solve_kernel(valid_ref, inverse_ref, right_ref, out_ref):
    solved = nt_dot(inverse_ref[...], right_ref[...]) * 0.5
    out_ref[...] = (solved * valid_ref[0:1, :]).astype(BF)


VMEM = pl.BlockSpec(memory_space=pltpu.VMEM)
SMEM = pl.BlockSpec(memory_space=pltpu.SMEM)


def call(kernel, out, ins, scratch=(), flops=0):
    return pl.pallas_call(
        kernel,
        out_shape=out,
        in_specs=ins,
        out_specs=jax.tree.map(lambda _: VMEM, out),
        scratch_shapes=list(scratch),
        compiler_params=pltpu.CompilerParams(vmem_limit_bytes=24 * 1024 * 1024),
        cost_estimate=pl.CostEstimate(flops=flops, bytes_accessed=2 * 1024 * 1024, transcendentals=0),
    )


def bf16(*shape):
    return jax.ShapeDtypeStruct(shape, BF)


def shards(forcing, legendre, assign, inverse, previous):
    rad, lat = lax.axis_index(RAD), lax.axis_index(LAT)
    orders = assign.reshape(1, 256)
    place = jnp.stack([rad * 4 + lat // 2, lat * 64 + rad]).astype(jnp.int32)

    sent = call(
        fourier_kernel, bf16(512, 1280), [VMEM] * 3, [pltpu.VMEM((512, LON), BF)], 2 * 512 * 768 * 1024
    )(orders, forcing, previous)
    sent, legendre = lax.optimization_barrier((sent, legendre))
    arrived = lax.all_to_all(sent, LAT + RAD, 0, 0, tiled=True)

    by_order = legendre.transpose(0, 2, 1)
    x = lax.axis_index("x")
    pieces = [lax.dynamic_index_in_dim(by_order, x, 0, keepdims=False)]
    for shift in range(1, 4):
        mine = lax.dynamic_index_in_dim(by_order, (x + shift) % 4, 0, keepdims=False)
        pieces.append(lax.ppermute(mine, "x", [(i, (i + shift) % 4) for i in range(4)]))
    stacked = jnp.stack(pieces)
    ordered = jnp.take(stacked, (x - jnp.arange(4)) % 4, axis=0)
    whole = lax.all_gather(ordered, "core", axis=0)
    weights = call(legendre_kernel, bf16(512, 1280), [VMEM, SMEM, VMEM], (), 2 * 512 * 512 * 768)(
        orders, place, whole
    )
    solver, valid = call(
        inverse_kernel,
        (bf16(512, 512), jax.ShapeDtypeStruct((8, 512), F32)),
        [VMEM, SMEM, VMEM],
        (),
        2 * 512**3,
    )(orders, place, inverse)

    right = call(
        spectrum_kernel, bf16(512, 512), [VMEM] * 2, [pltpu.VMEM((512, 1280), BF)], 2 * 512 * 512 * 1280
    )(arrived, weights)
    right = lax.all_to_all(right, RAD + LAT, 0, 0, tiled=True)
    solved = call(solve_kernel, bf16(512, 512), [VMEM] * 3, (), 2 * 512**3)(valid, solver, right)
    out = lax.all_to_all(solved.reshape(64, 8, 512), RAD, 0, 0, tiled=True)
    return out.transpose(1, 0, 2)


def solution(mesh):
    split = Mesh(mesh.devices.reshape(4, 2, 8, 8), LAT + RAD)
    placed = (
        P(RAD, LAT, None),
        P(RAD, None, LAT),
        P(),
        P(LAT + RAD, None, None),
        P(RAD, LAT, None),
    )
    return jax.shard_map(shards, mesh=split, in_specs=placed, out_specs=P(RAD, LAT, None), check_vma=False)
```

```python
import math

import jax
import jax.numpy as jnp
from jax import lax
from jax.experimental import pallas as pl
from jax.experimental.pallas import tpu as pltpu
from jax.sharding import Mesh, PartitionSpec as P

NR = 512
L = 512
LON = 1024
BF = jnp.bfloat16
F32 = jnp.float32
RAD = ("z", "y")
LAT = ("x", "core")


def nt_dot(a, b):
    return lax.dot_general(a, b, (((1,), (1,)), ((), ())), preferred_element_type=F32)


def iota(shape, dim):
    return lax.broadcasted_iota(jnp.int32, shape, dim)


def degree_of(row):
    return ((row >> 6) & 3) * 128 + (row >> 8) * 64 + (row & 63)


def cos_sin(phase):
    quadrant = ((phase + 128) >> 8) & 3
    rest = ((phase + 128) & 255) - 128
    x = rest.astype(F32) * (2.0 * math.pi / LON)
    x2 = x * x
    sin_x = x * (1.0 + x2 * (-1.0 / 6 + x2 * (1.0 / 120 + x2 * (-1.0 / 5040 + x2 * (1.0 / 362880)))))
    cos_x = 1.0 + x2 * (-0.5 + x2 * (1.0 / 24 + x2 * (-1.0 / 720 + x2 * (1.0 / 40320))))
    swap = (quadrant & 1) == 1
    cos_part = jnp.where(swap, sin_x, cos_x)
    sin_part = jnp.where(swap, cos_x, sin_x)
    cos_sign = jnp.where((quadrant == 1) | (quadrant == 2), -1.0, 1.0)
    sin_sign = jnp.where(quadrant >= 2, -1.0, 1.0)
    return cos_part * cos_sign, sin_part * sin_sign


def fourier_kernel(assign_ref, forcing_hbm, previous_hbm, out_ref, forcing_ref, previous_ref, table_ref, sems):
    forcing_copy = pltpu.make_async_copy(forcing_hbm, forcing_ref, sems.at[0])
    previous_copy = pltpu.make_async_copy(previous_hbm, previous_ref, sems.at[1])
    forcing_copy.start()
    previous_copy.start()
    row, lane = iota((512, 256), 0), iota((512, 256), 1)
    mine = lane == ((row >> 1) & 63) * 4 + (row >> 7)
    orders = jnp.sum(jnp.where(mine, assign_ref[...], 0), axis=1, keepdims=True)
    row, lane = iota((512, 128), 0), iota((512, 128), 1)
    cos_low, sin_low = cos_sin((orders * lane + (row & 1) * (LON // 4)) & (LON - 1))
    cos_high, sin_high = cos_sin((orders * 128 * lane) & (LON - 1))
    scale = LON**-0.5
    cos_low, sin_low = cos_low * scale, sin_low * scale
    for q in range(LON // 128):
        turned = cos_low * cos_high[:, q : q + 1] - sin_low * sin_high[:, q : q + 1]
        table_ref[:, q * 128 : q * 128 + 128] = turned.astype(BF)
    table = table_ref[...]
    row, column = iota((512, 512), 0), iota((512, 512), 1)
    reorder = (column == ((row >> 1) & 63) * 8 + (row >> 7) * 2 + (row & 1)).astype(BF)
    previous_copy.wait()
    before = nt_dot(reorder, previous_ref[...].reshape(512, 512)).astype(BF)
    forcing_copy.wait()
    parts = []
    for h in range(3):
        part = forcing_ref[:, h * 32 : h * 32 + 32, :].reshape(256, LON)
        parts.append(nt_dot(table, part).astype(BF))
    for half in range(2):
        pieces = [part[:, half * 128 : half * 128 + 128] for part in parts]
        pieces.append(before[:, half * 256 : half * 256 + 256])
        out_ref[half * 256 : half * 256 + 256] = jnp.concatenate(pieces, axis=1).reshape(256, 2, 640)


def legendre_kernel(assign_ref, place_ref, legendre_ref, out_ref):
    slot = place_ref[0]
    lane = iota((1, 256), 1)
    order = jnp.sum(jnp.where(lane == slot, assign_ref[...], 0), axis=1, keepdims=True)
    row, column = iota((512, 512), 0), iota((512, 512), 1)
    degree = degree_of(row)
    kept = jnp.where((column == degree) & (degree >= order), 1.0, 0.0).astype(BF)
    for h in range(3):
        for core in range(2):
            pieces = [legendre_ref[core, x, h * 32 : h * 32 + 32, :] for x in range(4)]
            at = h * 256 + core * 128
            out_ref[:, at : at + 128] = nt_dot(kept, jnp.concatenate(pieces, axis=0)).astype(BF)
    out_ref[:, 768:1280] = jnp.where(row == column, 2.0, 0.0).astype(BF)


def roll(a, shift):
    return pltpu.roll(a, shift, 1)


def spectrum_kernel(arrived_ref, weights_ref, out_ref, rows_ref, gathered_ref):
    rows_ref[...] = arrived_ref[...].reshape(1024, 640)
    lane = iota((128, 128), 1)
    low_half = lane < 64
    even_quarter = (lane & 32) == 0

    def tile(block, at):
        return rows_ref[block * 128 : block * 128 + 128, at : at + 128].astype(F32)

    def place(rho, at, value):
        gathered_ref[rho * 128 : rho * 128 + 128, at : at + 128] = value.astype(BF)

    for h in range(3):
        for core in range(2):
            a = [tile(core * 4 + x, h * 128) for x in range(4)]
            b0 = jnp.where(low_half, a[0], roll(a[2], 64))
            b2 = jnp.where(low_half, roll(a[0], 64), a[2])
            b1 = jnp.where(low_half, a[1], roll(a[3], 64))
            b3 = jnp.where(low_half, roll(a[1], 64), a[3])
            at = h * 256 + core * 128
            place(0, at, jnp.where(even_quarter, b0, roll(b1, 32)))
            place(1, at, jnp.where(even_quarter, roll(b0, 96), b1))
            place(2, at, jnp.where(even_quarter, b2, roll(b3, 32)))
            place(3, at, jnp.where(even_quarter, roll(b2, 96), b3))
    for pair in range(2):
        for two in range(4):
            at = 384 + pair * 128
            a0, a1 = tile(two * 2, at), tile(two * 2 + 1, at)
            to = 768 + two * 128
            place(pair * 2, to, jnp.where(low_half, a0, roll(a1, 64)))
            place(pair * 2 + 1, to, jnp.where(low_half, roll(a0, 64), a1))
    right = nt_dot(weights_ref[...], gathered_ref[...]).astype(BF)
    out_ref[...] = right.reshape(512, 2, 256)


def inverse_kernel(assign_ref, place_ref, inverse_ref, out_ref, valid_ref):
    inverse = inverse_ref[0].astype(BF)
    row, column = iota((512, 512), 0), iota((512, 512), 1)
    for c in range(2):
        for half in range(2):
            radius = ((row >> 1) & 63) * 8 + half * 4 + (row >> 7)
            spread = ((column == radius) & ((row & 1) == c)).astype(BF)
            out_ref[c * 2 + half] = nt_dot(inverse, spread).astype(BF)
    valid = jnp.where(assign_ref[...] <= place_ref[1], 1.0, 0.0)
    row, column = iota((256, 512), 0), iota((256, 512), 1)
    doubled = (row == (column >> 1)).astype(BF)
    valid_ref[...] = jnp.dot(
        jnp.broadcast_to(valid, (8, 256)).astype(BF), doubled, preferred_element_type=F32
    )


def solve_kernel(valid_ref, inverse_ref, right_ref, out_ref):
    right = right_ref[...].reshape(512, 512)
    parts = []
    for c in range(2):
        solved = nt_dot(inverse_ref[c * 2], right[:256]) + nt_dot(inverse_ref[c * 2 + 1], right[256:])
        parts.append((solved * 0.5).astype(BF))
    row, column = iota((512, 512), 0), iota((512, 512), 1)
    order = (column == (row & 63) * 8 + ((row >> 6) & 3) * 2 + (row >> 8)).astype(BF)
    solved = jnp.dot(jnp.concatenate(parts, axis=1), order, preferred_element_type=F32)
    out_ref[...] = (solved * valid_ref[0:1, :]).astype(BF)


VMEM = pl.BlockSpec(memory_space=pltpu.VMEM)
SMEM = pl.BlockSpec(memory_space=pltpu.SMEM)
HBM = pl.BlockSpec(memory_space=pltpu.HBM)


def call(kernel, out, ins, scratch=(), flops=0, vmem=24):
    return pl.pallas_call(
        kernel,
        out_shape=out,
        in_specs=ins,
        out_specs=jax.tree.map(lambda _: VMEM, out),
        scratch_shapes=list(scratch),
        compiler_params=pltpu.CompilerParams(vmem_limit_bytes=vmem * 1024 * 1024),
        cost_estimate=pl.CostEstimate(flops=flops, bytes_accessed=2 * 1024 * 1024, transcendentals=0),
    )


def bf16(*shape):
    return jax.ShapeDtypeStruct(shape, BF)


def shards(forcing, legendre, assign, inverse, previous):
    rad, lat = lax.axis_index(RAD), lax.axis_index(LAT)
    orders = assign.reshape(1, 256)
    place = jnp.stack([rad * 4 + lat // 2, lat * 64 + rad]).astype(jnp.int32)

    sent = call(
        fourier_kernel,
        bf16(512, 2, 640),
        [VMEM, HBM, HBM],
        [
            pltpu.VMEM((8, 96, LON), BF),
            pltpu.VMEM((8, 64, 512), BF),
            pltpu.VMEM((512, LON), BF),
            pltpu.SemaphoreType.DMA((2,)),
        ],
        2 * 512 * 768 * 1024,
        60,
    )(orders, forcing, previous)
    sent, legendre = lax.optimization_barrier((sent, legendre))
    arrived = lax.all_to_all(sent, ("core", "x") + RAD, 0, 0, tiled=True)

    by_order = legendre.transpose(0, 2, 1)
    x = lax.axis_index("x")
    pieces = [lax.dynamic_index_in_dim(by_order, x, 0, keepdims=False)]
    for shift in range(1, 4):
        mine = lax.dynamic_index_in_dim(by_order, (x + shift) % 4, 0, keepdims=False)
        pieces.append(lax.ppermute(mine, "x", [(i, (i + shift) % 4) for i in range(4)]))
    stacked = jnp.stack(pieces)
    ordered = jnp.take(stacked, (x - jnp.arange(4)) % 4, axis=0)
    whole = lax.all_gather(ordered, "core", axis=0)
    weights = call(legendre_kernel, bf16(512, 1280), [VMEM, SMEM, VMEM], (), 2 * 512 * 512 * 768)(
        orders, place, whole
    )
    solver, valid = call(
        inverse_kernel,
        (bf16(4, 512, 512), jax.ShapeDtypeStruct((8, 512), F32)),
        [VMEM, SMEM, VMEM],
        (),
        2 * 512**3,
    )(orders, place, inverse)

    right = call(
        spectrum_kernel,
        bf16(512, 2, 256),
        [VMEM] * 2,
        [pltpu.VMEM((1024, 640), BF), pltpu.VMEM((512, 1280), BF)],
        2 * 512 * 512 * 1280,
    )(arrived, weights)
    right = lax.all_to_all(right, ("core", "x") + RAD, 0, 0, tiled=True)
    solved = call(solve_kernel, bf16(512, 512), [VMEM] * 3, (), 2 * 512**3)(valid, solver, right)
    out = lax.all_to_all(solved.reshape(64, 8, 512), RAD, 0, 0, tiled=True)
    return out.transpose(1, 0, 2)


def solution(mesh):
    split = Mesh(mesh.devices.reshape(4, 2, 8, 8), LAT + RAD)
    placed = (
        P(RAD, LAT, None),
        P(RAD, None, LAT),
        P(),
        P(LAT + RAD, None, None),
        P(RAD, LAT, None),
    )
    return jax.shard_map(shards, mesh=split, in_specs=placed, out_specs=P(RAD, LAT, None), check_vma=False)
```

```python
import math

import jax
import jax.numpy as jnp
from jax import lax
from jax.experimental import pallas as pl
from jax.experimental.pallas import tpu as pltpu
from jax.sharding import Mesh, PartitionSpec as P

NR = 512
L = 512
LON = 1024
BF = jnp.bfloat16
F32 = jnp.float32
RAD = ("zh", "zl", "y")
LAT = ("x", "core")


def nt_dot(a, b):
    return lax.dot_general(a, b, (((1,), (1,)), ((), ())), preferred_element_type=F32)


def iota(shape, dim):
    return lax.broadcasted_iota(jnp.int32, shape, dim)


def cos_sin(phase):
    quadrant = ((phase + 128) >> 8) & 3
    rest = ((phase + 128) & 255) - 128
    x = rest.astype(F32) * (2.0 * math.pi / LON)
    x2 = x * x
    sin_x = x * (1.0 + x2 * (-1.0 / 6 + x2 * (1.0 / 120 + x2 * (-1.0 / 5040 + x2 * (1.0 / 362880)))))
    cos_x = 1.0 + x2 * (-0.5 + x2 * (1.0 / 24 + x2 * (-1.0 / 720 + x2 * (1.0 / 40320))))
    swap = (quadrant & 1) == 1
    cos_part = jnp.where(swap, sin_x, cos_x)
    sin_part = jnp.where(swap, cos_x, sin_x)
    cos_sign = jnp.where((quadrant == 1) | (quadrant == 2), -1.0, 1.0)
    sin_sign = jnp.where(quadrant >= 2, -1.0, 1.0)
    return cos_part * cos_sign, sin_part * sin_sign


def fourier_kernel(
    assign_ref, forcing_hbm, previous_hbm, out_hbm, forcing_ref, previous_ref, table_ref, out_ref, in_sems, out_sems
):
    previous_copy = pltpu.make_async_copy(previous_hbm, previous_ref, in_sems.at[3])
    previous_copy.start()
    forcing_copies = []
    for h in range(3):
        part = pl.ds(h * 32, 32)
        copy = pltpu.make_async_copy(forcing_hbm.at[:, part, :], forcing_ref.at[:, part, :], in_sems.at[h])
        copy.start()
        forcing_copies.append(copy)
    row = iota((512, 1), 0)
    slot = ((row >> 4) & 3) * 64 + (row >> 8) * 32 + ((row >> 1) & 7) * 4 + ((row >> 6) & 3)
    orders = jnp.sum(jnp.where(iota((512, 256), 1) == slot, assign_ref[...], 0), axis=1, keepdims=True)
    lane = iota((512, 128), 1)
    cos_low, sin_low = cos_sin((orders * lane + (row & 1) * (LON // 4)) & (LON - 1))
    cos_high, sin_high = cos_sin((orders * 128 * lane) & (LON - 1))
    scale = LON**-0.5
    cos_low, sin_low = cos_low * scale, sin_low * scale
    for q in range(LON // 128):
        turned = cos_low * cos_high[:, q : q + 1] - sin_low * sin_high[:, q : q + 1]
        table_ref[:, q * 128 : q * 128 + 128] = turned.astype(BF)
    table = table_ref[...]
    reorder = (iota((512, 512), 1) == slot * 2 + (row & 1)).astype(BF)
    out_copies = []

    def send(at, width, value):
        out_ref[:, :, at : at + width] = value.astype(BF).reshape(256, 2, width)
        part = pl.ds(at, width)
        copy = pltpu.make_async_copy(out_ref.at[:, :, part], out_hbm.at[:, :, part], out_sems.at[len(out_copies)])
        copy.start()
        out_copies.append(copy)

    previous_copy.wait()
    send(768, 512, nt_dot(reorder, previous_ref[...].reshape(512, 512)))
    for h in range(3):
        forcing_copies[h].wait()
        part = forcing_ref[:, h * 32 : h * 32 + 32, :].reshape(256, LON)
        send(h * 256, 256, nt_dot(table, part))
    for copy in out_copies:
        copy.wait()


def legendre_kernel(assign_ref, place_ref, legendre_ref, out_ref, parted_ref):
    order = jnp.sum(jnp.where(iota((1, 256), 1) == place_ref[0], assign_ref[...], 0), axis=1, keepdims=True)
    row = iota((512, 1), 0)
    core, x = (row >> 5) & 1, row & 3
    inner = ((row >> 6) & 3) * 16 + (row >> 8) * 8 + ((row >> 2) & 7)
    degree = (2 * x + core) * 64 + inner
    column = iota((512, 512), 1)
    kept = jnp.where((column == degree) & (degree >= order), 1.0, 0.0).astype(BF)
    for h in range(3):
        for core_from in range(2):
            pieces = [legendre_ref[core_from, x_from, h * 32 : h * 32 + 32, :] for x_from in range(4)]
            at = h * 256 + core_from * 128
            out_ref[:, at : at + 128] = nt_dot(kept, jnp.concatenate(pieces, axis=0)).astype(BF)
    out_ref[:, 768:1280] = jnp.where(column == core * 256 + x * 64 + inner, 2.0, 0.0).astype(BF)
    parted_ref[...] = (column == (row & 1) * 256 + (row >> 1)).astype(BF)


def roll(a, shift):
    return pltpu.roll(a, shift, 1)


def spectrum_kernel(arrived_ref, weights_ref, parted_ref, out_ref, gathered_ref):
    lane = iota((64, 128), 1)
    low_half = lane < 64
    even_quarter = (lane & 32) == 0

    def tile(block, at):
        return arrived_ref[block * 32 : block * 32 + 32, :, at : at + 128].reshape(64, 128).astype(F32)

    def place(rho, at, value):
        gathered_ref[rho * 64 : rho * 64 + 64, at : at + 128] = value.astype(BF)

    for h in range(3):
        for high in range(2):
            for core in range(2):
                a = [tile(core * 4 + x, h * 256 + high * 128) for x in range(4)]
                b0 = jnp.where(low_half, a[0], roll(a[2], 64))
                b2 = jnp.where(low_half, roll(a[0], 64), a[2])
                b1 = jnp.where(low_half, a[1], roll(a[3], 64))
                b3 = jnp.where(low_half, roll(a[1], 64), a[3])
                at, rho = h * 256 + core * 128, high * 4
                place(rho, at, jnp.where(even_quarter, b0, roll(b1, 32)))
                place(rho + 1, at, jnp.where(even_quarter, roll(b0, 96), b1))
                place(rho + 2, at, jnp.where(even_quarter, b2, roll(b3, 32)))
                place(rho + 3, at, jnp.where(even_quarter, roll(b2, 96), b3))
    for pair in range(4):
        for two in range(4):
            at = 768 + pair * 128
            a0, a1 = tile(two * 2, at), tile(two * 2 + 1, at)
            to = 768 + two * 128
            place(pair * 2, to, jnp.where(low_half, a0, roll(a1, 64)))
            place(pair * 2 + 1, to, jnp.where(low_half, roll(a0, 64), a1))
    right = nt_dot(weights_ref[...], gathered_ref[...]).astype(BF)
    right = jnp.dot(right, parted_ref[...], preferred_element_type=F32).astype(BF)
    out_ref[...] = right.reshape(512, 2, 256)


def inverse_kernel(assign_ref, place_ref, inverse_ref, out_ref, valid_ref):
    inverse = inverse_ref[0].astype(BF)
    row, column = iota((256, 512), 0), iota((256, 512), 1)
    for zl in range(2):
        radius = ((row >> 3) & 3) * 128 + zl * 64 + (row & 7) * 8 + (row >> 5)
        out_ref[zl] = nt_dot(inverse, (column == radius).astype(BF)).astype(BF)
    valid = jnp.where(assign_ref[...] <= place_ref[1], 1.0, 0.0)
    doubled = (row == (column >> 1)).astype(BF)
    valid_ref[...] = jnp.dot(
        jnp.broadcast_to(valid, (8, 256)).astype(BF), doubled, preferred_element_type=F32
    )


def solve_kernel(valid_ref, inverse_ref, right_ref, out_ref):
    right = right_ref[...].reshape(1024, 256)
    solved = nt_dot(inverse_ref[0], right[:512]) + nt_dot(inverse_ref[1], right[512:])
    out_ref[...] = (solved * (valid_ref[0:1, :] * 0.5)).astype(BF)


VMEM = pl.BlockSpec(memory_space=pltpu.VMEM)
SMEM = pl.BlockSpec(memory_space=pltpu.SMEM)
HBM = pl.BlockSpec(memory_space=pltpu.HBM)


def call(kernel, out, ins, scratch=(), flops=0, vmem=24, outs=None):
    return pl.pallas_call(
        kernel,
        out_shape=out,
        in_specs=ins,
        out_specs=outs or jax.tree.map(lambda _: VMEM, out),
        scratch_shapes=list(scratch),
        compiler_params=pltpu.CompilerParams(vmem_limit_bytes=vmem * 1024 * 1024),
        cost_estimate=pl.CostEstimate(flops=flops, bytes_accessed=2 * 1024 * 1024, transcendentals=0),
    )


def bf16(*shape):
    return jax.ShapeDtypeStruct(shape, BF)


def shards(forcing, legendre, assign, inverse, previous):
    x, core = lax.axis_index("x"), lax.axis_index("core")
    zh, zl, y = lax.axis_index("zh"), lax.axis_index("zl"), lax.axis_index("y")
    orders = assign.reshape(1, 256)
    slot = zh * 64 + core * 32 + y * 4 + x
    degree = (x * 2 + core) * 64 + zh * 16 + zl * 8 + y
    place = jnp.stack([slot, degree]).astype(jnp.int32)

    sent = call(
        fourier_kernel,
        bf16(256, 2, 1280),
        [VMEM, HBM, HBM],
        [
            pltpu.VMEM((8, 96, LON), BF),
            pltpu.VMEM((8, 64, 512), BF),
            pltpu.VMEM((512, LON), BF),
            pltpu.VMEM((256, 2, 1280), BF),
            pltpu.SemaphoreType.DMA((4,)),
            pltpu.SemaphoreType.DMA((4,)),
        ],
        2 * 512 * 768 * 1024,
        60,
        HBM,
    )(orders, forcing, previous)
    sent, legendre = lax.optimization_barrier((sent, legendre))
    arrived = lax.all_to_all(sent, ("core", "x", "zh", "y"), 0, 0, tiled=True)

    by_order = legendre.transpose(0, 2, 1)
    pieces = [lax.dynamic_index_in_dim(by_order, x, 0, keepdims=False)]
    for shift in range(1, 4):
        mine = lax.dynamic_index_in_dim(by_order, (x + shift) % 4, 0, keepdims=False)
        pieces.append(lax.ppermute(mine, "x", [(i, (i + shift) % 4) for i in range(4)]))
    stacked = jnp.stack(pieces)
    ordered = jnp.take(stacked, (x - jnp.arange(4)) % 4, axis=0)
    whole = lax.all_gather(ordered, "core", axis=0)
    other = lax.ppermute(whole, ("core", "zl"), [(0, 1), (3, 2)])
    whole = jnp.where(core == zl, whole, other)
    weights, parted = call(
        legendre_kernel, (bf16(512, 1280), bf16(512, 512)), [VMEM, SMEM, VMEM], (), 2 * 512 * 512 * 768
    )(orders, place, whole)
    solver, valid = call(
        inverse_kernel,
        (bf16(2, 512, 256), jax.ShapeDtypeStruct((8, 512), F32)),
        [VMEM, SMEM, VMEM],
        (),
        2 * 512**3,
    )(orders, place, inverse)

    right = call(
        spectrum_kernel,
        bf16(512, 2, 256),
        [VMEM] * 3,
        [pltpu.VMEM((512, 1280), BF)],
        2 * 512 * 512 * 1792,
    )(arrived, weights, parted)
    right = lax.all_to_all(right, ("zl", "zh", "core", "y", "x"), 0, 0, tiled=True)
    solved = call(solve_kernel, bf16(512, 512), [VMEM] * 3, (), 2 * 512**3)(valid, solver, right)
    out = lax.all_to_all(solved.reshape(64, 8, 512), RAD, 0, 0, tiled=True)
    return out.transpose(1, 0, 2)


def solution(mesh):
    split = Mesh(mesh.devices.reshape(4, 2, 4, 2, 8), LAT + RAD)
    placed = (
        P(RAD, LAT, None),
        P(RAD, None, LAT),
        P(),
        P(LAT + RAD, None, None),
        P(RAD, LAT, None),
    )
    return jax.shard_map(shards, mesh=split, in_specs=placed, out_specs=P(RAD, LAT, None), check_vma=False)
```

```python
import math

import jax
import jax.numpy as jnp
from jax import lax
from jax.experimental import pallas as pl
from jax.experimental.pallas import tpu as pltpu
from jax.sharding import Mesh, PartitionSpec as P

NR = 512
L = 512
LON = 1024
BF = jnp.bfloat16
F32 = jnp.float32
RAD = ("zh", "zl", "y")
LAT = ("x", "core")


def nt_dot(a, b):
    return lax.dot_general(a, b, (((1,), (1,)), ((), ())), preferred_element_type=F32)


def iota(shape, dim):
    return lax.broadcasted_iota(jnp.int32, shape, dim)


def cos_sin(phase):
    quadrant = ((phase + 128) >> 8) & 3
    rest = ((phase + 128) & 255) - 128
    x = rest.astype(F32) * (2.0 * math.pi / LON)
    x2 = x * x
    sin_x = x * (1.0 + x2 * (-1.0 / 6 + x2 * (1.0 / 120 + x2 * (-1.0 / 5040 + x2 * (1.0 / 362880)))))
    cos_x = 1.0 + x2 * (-0.5 + x2 * (1.0 / 24 + x2 * (-1.0 / 720 + x2 * (1.0 / 40320))))
    swap = (quadrant & 1) == 1
    cos_part = jnp.where(swap, sin_x, cos_x)
    sin_part = jnp.where(swap, cos_x, sin_x)
    cos_sign = jnp.where((quadrant == 1) | (quadrant == 2), -1.0, 1.0)
    sin_sign = jnp.where(quadrant >= 2, -1.0, 1.0)
    return cos_part * cos_sign, sin_part * sin_sign


def fourier_kernel(
    assign_ref, forcing_hbm, previous_hbm, out_hbm, forcing_ref, previous_ref, table_ref, out_ref, in_sems, out_sems
):
    previous_copy = pltpu.make_async_copy(previous_hbm, previous_ref, in_sems.at[1])
    previous_copy.start()
    forcing_copy = pltpu.make_async_copy(forcing_hbm, forcing_ref, in_sems.at[0])
    forcing_copy.start()
    row = iota((512, 1), 0)
    slot = ((row >> 4) & 3) * 64 + (row >> 8) * 32 + ((row >> 1) & 7) * 4 + ((row >> 6) & 3)
    orders = jnp.sum(jnp.where(iota((512, 256), 1) == slot, assign_ref[...], 0), axis=1, keepdims=True)
    lane = iota((512, 128), 1)
    cos_now, sin_now = cos_sin((orders * lane + (row & 1) * (LON // 4)) & (LON - 1))
    cos_half, sin_half = cos_now[:, 64:65], sin_now[:, 64:65]
    sign = (1 - 2 * (row & 1)).astype(F32)
    cos_step = jnp.broadcast_to(sign * (1.0 - 2.0 * sin_half * sin_half), (512, 128))
    sin_step = jnp.broadcast_to(sign * (2.0 * sin_half * cos_half), (512, 128))
    cos_now, sin_now = cos_now * LON**-0.5, sin_now * LON**-0.5
    for q in range(LON // 128):
        table_ref[:, q * 128 : q * 128 + 128] = cos_now.astype(BF)
        cos_now, sin_now = cos_now * cos_step - sin_now * sin_step, sin_now * cos_step + cos_now * sin_step
    table = table_ref[...]
    reorder = (iota((512, 512), 1) == slot * 2 + (row & 1)).astype(BF)
    previous_copy.wait()
    previous = previous_ref[...].reshape(512, 512)
    forcing_copy.wait()
    out_copies = []
    for block in range(2):
        rows = slice(block * 256, block * 256 + 256)
        dests = pl.ds(block * 128, 128)
        for h in range(3):
            part = forcing_ref[:, h * 32 : h * 32 + 32, :].reshape(256, LON)
            part = nt_dot(table[rows], part).astype(BF)
            out_ref[dests, :, h * 256 : h * 256 + 256] = part.reshape(128, 2, 256)
        out_ref[dests, :, 768:1280] = nt_dot(reorder[rows], previous).astype(BF).reshape(128, 2, 512)
        copy = pltpu.make_async_copy(out_ref.at[dests], out_hbm.at[dests], out_sems.at[block])
        copy.start()
        out_copies.append(copy)
    for copy in out_copies:
        copy.wait()


def legendre_kernel(assign_ref, place_ref, same_ref, crossed_ref, out_ref, parted_ref):
    order = jnp.sum(jnp.where(iota((1, 256), 1) == place_ref[0], assign_ref[...], 0), axis=1, keepdims=True)
    row = iota((512, 1), 0)
    core, x = (row >> 5) & 1, row & 3
    inner = ((row >> 6) & 3) * 16 + (row >> 8) * 8 + ((row >> 2) & 7)
    degree = (2 * x + core) * 64 + inner
    column = iota((512, 512), 1)
    kept = jnp.where((column == degree) & (degree >= order), 1.0, 0.0).astype(BF)
    x_here, straight = place_ref[2], place_ref[3] == 0
    for h in range(3):
        rows = pl.ds(h * 32, 32)
        for core_from in range(2):
            pieces = []
            for x_from in range(4):
                at = (x_here - x_from) & 3
                near, far = same_ref[at, rows, :], crossed_ref[at, rows, :]
                pieces.append(jnp.where(straight == (core_from == 0), near, far))
            at = h * 256 + core_from * 128
            out_ref[:, at : at + 128] = nt_dot(kept, jnp.concatenate(pieces, axis=0)).astype(BF)
    out_ref[:, 768:1280] = jnp.where(column == core * 256 + x * 64 + inner, 2.0, 0.0).astype(BF)
    parted_ref[...] = (column == (row & 1) * 256 + (row >> 1)).astype(BF)


def roll(a, shift):
    return pltpu.roll(a, shift, 1)


def spectrum_kernel(arrived_ref, weights_ref, parted_ref, out_ref, rows_ref, gathered_ref):
    rows_ref[...] = arrived_ref[...].reshape(512, 1280)
    lane = iota((64, 128), 1)
    low_half = lane < 64
    even_quarter = (lane & 32) == 0

    def tile(block, at):
        return rows_ref[block * 64 : block * 64 + 64, at : at + 128].astype(F32)

    def place(rho, at, value):
        gathered_ref[rho * 64 : rho * 64 + 64, at : at + 128] = value.astype(BF)

    for h in range(3):
        for high in range(2):
            for core in range(2):
                a = [tile(core * 4 + x, h * 256 + high * 128) for x in range(4)]
                b0 = jnp.where(low_half, a[0], roll(a[2], 64))
                b2 = jnp.where(low_half, roll(a[0], 64), a[2])
                b1 = jnp.where(low_half, a[1], roll(a[3], 64))
                b3 = jnp.where(low_half, roll(a[1], 64), a[3])
                at, rho = h * 256 + core * 128, high * 4
                place(rho, at, jnp.where(even_quarter, b0, roll(b1, 32)))
                place(rho + 1, at, jnp.where(even_quarter, roll(b0, 96), b1))
                place(rho + 2, at, jnp.where(even_quarter, b2, roll(b3, 32)))
                place(rho + 3, at, jnp.where(even_quarter, roll(b2, 96), b3))
    for pair in range(4):
        for two in range(4):
            at = 768 + pair * 128
            a0, a1 = tile(two * 2, at), tile(two * 2 + 1, at)
            to = 768 + two * 128
            place(pair * 2, to, jnp.where(low_half, a0, roll(a1, 64)))
            place(pair * 2 + 1, to, jnp.where(low_half, roll(a0, 64), a1))
    right = nt_dot(weights_ref[...], gathered_ref[...]).astype(BF)
    right = jnp.dot(right, parted_ref[...], preferred_element_type=F32).astype(BF)
    out_ref[...] = right.reshape(512, 2, 256)


def inverse_kernel(assign_ref, place_ref, inverse_ref, out_ref, valid_ref):
    inverse = inverse_ref[0].astype(BF)
    row, column = iota((256, 512), 0), iota((256, 512), 1)
    for zl in range(2):
        radius = ((row >> 3) & 3) * 128 + zl * 64 + (row & 7) * 8 + (row >> 5)
        out_ref[zl] = nt_dot(inverse, (column == radius).astype(BF)).astype(BF)
    valid = jnp.where(assign_ref[...] <= place_ref[1], 1.0, 0.0)
    doubled = (row == (column >> 1)).astype(BF)
    valid_ref[...] = jnp.dot(
        jnp.broadcast_to(valid, (8, 256)).astype(BF), doubled, preferred_element_type=F32
    )


def solve_kernel(valid_ref, inverse_ref, right_ref, out_ref):
    right = right_ref[...].reshape(1024, 256)
    solved = nt_dot(inverse_ref[0], right[:512]) + nt_dot(inverse_ref[1], right[512:])
    out_ref[...] = (solved * (valid_ref[0:1, :] * 0.5)).astype(BF)


VMEM = pl.BlockSpec(memory_space=pltpu.VMEM)
SMEM = pl.BlockSpec(memory_space=pltpu.SMEM)
HBM = pl.BlockSpec(memory_space=pltpu.HBM)


def call(kernel, out, ins, scratch=(), flops=0, vmem=24, outs=None):
    return pl.pallas_call(
        kernel,
        out_shape=out,
        in_specs=ins,
        out_specs=outs or jax.tree.map(lambda _: VMEM, out),
        scratch_shapes=list(scratch),
        compiler_params=pltpu.CompilerParams(vmem_limit_bytes=vmem * 1024 * 1024),
        cost_estimate=pl.CostEstimate(flops=flops, bytes_accessed=2 * 1024 * 1024, transcendentals=0),
    )


def bf16(*shape):
    return jax.ShapeDtypeStruct(shape, BF)


def shards(forcing, legendre, assign, inverse, previous):
    x, core = lax.axis_index("x"), lax.axis_index("core")
    zh, zl, y = lax.axis_index("zh"), lax.axis_index("zl"), lax.axis_index("y")
    orders = assign.reshape(1, 256)
    slot = zh * 64 + core * 32 + y * 4 + x
    degree = (x * 2 + core) * 64 + zh * 16 + zl * 8 + y
    place = jnp.stack([slot, degree, x, zl]).astype(jnp.int32)

    sent = call(
        fourier_kernel,
        bf16(256, 2, 1280),
        [VMEM, HBM, HBM],
        [
            pltpu.VMEM((8, 96, LON), BF),
            pltpu.VMEM((8, 64, 512), BF),
            pltpu.VMEM((512, LON), BF),
            pltpu.VMEM((256, 2, 1280), BF),
            pltpu.SemaphoreType.DMA((2,)),
            pltpu.SemaphoreType.DMA((2,)),
        ],
        2 * 512 * 768 * 1024,
        60,
        HBM,
    )(orders, forcing, previous)
    sent, legendre = lax.optimization_barrier((sent, legendre))
    arrived = lax.all_to_all(sent, ("core", "x", "zh", "y"), 0, 0, tiled=True)

    by_order = legendre.transpose(0, 2, 1)
    rolled = jnp.take(by_order, (x + jnp.arange(4)) % 4, axis=0)
    two_on = lax.ppermute(rolled[2:], "x", [(i, (i + 2) % 4) for i in range(4)])
    one_on = jnp.stack([rolled[1], two_on[1]])
    one_on = lax.ppermute(one_on, "x", [(i, (i + 1) % 4) for i in range(4)])
    gathered = jnp.stack([rolled[0], one_on[0], two_on[0], one_on[1]])
    same = lax.ppermute(gathered, ("core", "zl"), [(0, 0), (1, 2), (2, 1), (3, 3)])
    crossed = lax.ppermute(gathered, ("core", "zl"), [(0, 1), (1, 3), (2, 0), (3, 2)])
    weights, parted = call(
        legendre_kernel, (bf16(512, 1280), bf16(512, 512)), [VMEM, SMEM, VMEM, VMEM], (), 2 * 512 * 512 * 768
    )(orders, place, same, crossed)
    solver, valid = call(
        inverse_kernel,
        (bf16(2, 512, 256), jax.ShapeDtypeStruct((8, 512), F32)),
        [VMEM, SMEM, VMEM],
        (),
        2 * 512**3,
    )(orders, place, inverse)

    right = call(
        spectrum_kernel,
        bf16(512, 2, 256),
        [VMEM] * 3,
        [pltpu.VMEM((512, 1280), BF)] * 2,
        2 * 512 * 512 * 1792,
    )(arrived, weights, parted)
    right = lax.all_to_all(right, ("zl", "zh", "core", "y", "x"), 0, 0, tiled=True)
    solved = call(solve_kernel, bf16(512, 512), [VMEM] * 3, (), 2 * 512**3)(valid, solver, right)
    out = lax.all_to_all(solved.reshape(64, 8, 512), RAD, 0, 0, tiled=True)
    return out.transpose(1, 0, 2)


def solution(mesh):
    split = Mesh(mesh.devices.reshape(4, 2, 4, 2, 8), LAT + RAD)
    placed = (
        P(RAD, LAT, None),
        P(RAD, None, LAT),
        P(),
        P(LAT + RAD, None, None),
        P(RAD, LAT, None),
    )
    return jax.shard_map(shards, mesh=split, in_specs=placed, out_specs=P(RAD, LAT, None), check_vma=False)
```

```python
import math

import jax
import jax.numpy as jnp
from jax import lax
from jax.experimental import pallas as pl
from jax.experimental.pallas import tpu as pltpu
from jax.sharding import Mesh, PartitionSpec as P

NR = 512
L = 512
LON = 1024
BF = jnp.bfloat16
F32 = jnp.float32
RAD = ("z", "y")
LAT = ("x", "core")


def nt_dot(a, b):
    return lax.dot_general(a, b, (((1,), (1,)), ((), ())), preferred_element_type=F32)


def iota(shape, dim):
    return lax.broadcasted_iota(jnp.int32, shape, dim)


def cos_sin(phase):
    quadrant = ((phase + 128) >> 8) & 3
    rest = ((phase + 128) & 255) - 128
    x = rest.astype(F32) * (2.0 * math.pi / LON)
    x2 = x * x
    sin_x = x * (1.0 + x2 * (-1.0 / 6 + x2 * (1.0 / 120 + x2 * (-1.0 / 5040 + x2 * (1.0 / 362880)))))
    cos_x = 1.0 + x2 * (-0.5 + x2 * (1.0 / 24 + x2 * (-1.0 / 720 + x2 * (1.0 / 40320))))
    swap = (quadrant & 1) == 1
    cos_part = jnp.where(swap, sin_x, cos_x)
    sin_part = jnp.where(swap, cos_x, sin_x)
    cos_sign = jnp.where((quadrant == 1) | (quadrant == 2), -1.0, 1.0)
    sin_sign = jnp.where(quadrant >= 2, -1.0, 1.0)
    return cos_part * cos_sign, sin_part * sin_sign


def fourier_kernel(
    assign_ref, forcing_hbm, previous_hbm, out_hbm, forcing_ref, previous_ref, table_ref, out_ref, in_sems, out_sems
):
    previous_copy = pltpu.make_async_copy(previous_hbm, previous_ref, in_sems.at[1])
    previous_copy.start()
    forcing_copy = pltpu.make_async_copy(forcing_hbm, forcing_ref, in_sems.at[0])
    forcing_copy.start()
    row = iota((512, 1), 0)
    slot = ((row >> 1) & 63) * 4 + (row >> 7)
    orders = jnp.sum(jnp.where(iota((512, 256), 1) == slot, assign_ref[...], 0), axis=1, keepdims=True)
    lane = iota((512, 128), 1)
    cos_now, sin_now = cos_sin((orders * lane + (row & 1) * (LON // 4)) & (LON - 1))
    cos_half, sin_half = cos_now[:, 64:65], sin_now[:, 64:65]
    sign = (1 - 2 * (row & 1)).astype(F32)
    cos_step = jnp.broadcast_to(sign * (1.0 - 2.0 * sin_half * sin_half), (512, 128))
    sin_step = jnp.broadcast_to(sign * (2.0 * sin_half * cos_half), (512, 128))
    cos_now, sin_now = cos_now * LON**-0.5, sin_now * LON**-0.5
    for q in range(LON // 128):
        table_ref[:, q * 128 : q * 128 + 128] = cos_now.astype(BF)
        cos_now, sin_now = cos_now * cos_step - sin_now * sin_step, sin_now * cos_step + cos_now * sin_step
    table = table_ref[...]
    reorder = (iota((512, 512), 1) == slot * 2 + (row & 1)).astype(BF)
    previous_copy.wait()
    previous = previous_ref[...].reshape(512, 512)
    forcing_copy.wait()
    out_copies = []
    for block in range(2):
        rows = slice(block * 256, block * 256 + 256)
        parts = []
        for h in range(3):
            part = forcing_ref[:, h * 32 : h * 32 + 32, :].reshape(256, LON)
            parts.append(nt_dot(table[rows], part).astype(BF))
        before = nt_dot(reorder[rows], previous).astype(BF)
        for half in range(2):
            dests = pl.ds(half * 256 + block * 128, 128)
            pieces = [part[:, half * 128 : half * 128 + 128] for part in parts]
            pieces.append(before[:, half * 256 : half * 256 + 256])
            out_ref[dests] = jnp.concatenate(pieces, axis=1).reshape(128, 2, 640)
            sem = out_sems.at[block * 2 + half]
            copy = pltpu.make_async_copy(out_ref.at[dests], out_hbm.at[dests], sem)
            copy.start()
            out_copies.append(copy)
    for copy in out_copies:
        copy.wait()


def legendre_kernel(assign_ref, place_ref, legendre_ref, out_ref, parted_ref):
    order = jnp.sum(jnp.where(iota((1, 256), 1) == place_ref[0], assign_ref[...], 0), axis=1, keepdims=True)
    row = iota((512, 1), 0)
    core, x, inner = row >> 8, row & 3, (row >> 2) & 63
    degree = (2 * x + core) * 64 + inner
    column = iota((512, 512), 1)
    kept = jnp.where((column == degree) & (degree >= order), 1.0, 0.0).astype(BF)
    x_here = place_ref[2]
    for h in range(3):
        rows = pl.ds(h * 32, 32)
        for core_from in range(2):
            pieces = [legendre_ref[core_from, (x_here - x_from) & 3, rows, :] for x_from in range(4)]
            at = h * 256 + core_from * 128
            out_ref[:, at : at + 128] = nt_dot(kept, jnp.concatenate(pieces, axis=0)).astype(BF)
    out_ref[:, 768:1280] = jnp.where(column == core * 256 + x * 64 + inner, 2.0, 0.0).astype(BF)
    parted_ref[...] = (column == (row & 1) * 256 + (row >> 1)).astype(BF)


def roll(a, shift):
    return pltpu.roll(a, shift, 1)


def spectrum_kernel(arrived_ref, weights_ref, parted_ref, out_ref, rows_ref, gathered_ref):
    rows_ref[...] = arrived_ref[...].reshape(1024, 640)
    lane = iota((128, 128), 1)
    low_half = lane < 64
    even_quarter = (lane & 32) == 0

    def tile(block, at):
        return rows_ref[block * 128 : block * 128 + 128, at : at + 128].astype(F32)

    def place(rho, at, value):
        gathered_ref[rho * 128 : rho * 128 + 128, at : at + 128] = value.astype(BF)

    for h in range(3):
        for core in range(2):
            a = [tile(core * 4 + x, h * 128) for x in range(4)]
            b0 = jnp.where(low_half, a[0], roll(a[2], 64))
            b2 = jnp.where(low_half, roll(a[0], 64), a[2])
            b1 = jnp.where(low_half, a[1], roll(a[3], 64))
            b3 = jnp.where(low_half, roll(a[1], 64), a[3])
            at = h * 256 + core * 128
            place(0, at, jnp.where(even_quarter, b0, roll(b1, 32)))
            place(1, at, jnp.where(even_quarter, roll(b0, 96), b1))
            place(2, at, jnp.where(even_quarter, b2, roll(b3, 32)))
            place(3, at, jnp.where(even_quarter, roll(b2, 96), b3))
    for pair in range(2):
        for two in range(4):
            at = 384 + pair * 128
            a0, a1 = tile(two * 2, at), tile(two * 2 + 1, at)
            to = 768 + two * 128
            place(pair * 2, to, jnp.where(low_half, a0, roll(a1, 64)))
            place(pair * 2 + 1, to, jnp.where(low_half, roll(a0, 64), a1))
    right = nt_dot(weights_ref[...], gathered_ref[...]).astype(BF)
    right = jnp.dot(right, parted_ref[...], preferred_element_type=F32).astype(BF)
    out_ref[...] = right.reshape(512, 2, 256)


def inverse_kernel(assign_ref, place_ref, inverse_ref, out_ref, valid_ref):
    inverse = inverse_ref[0].astype(BF)
    row, column = iota((256, 512), 0), iota((256, 512), 1)
    for half in range(2):
        radius = (row & 63) * 8 + half * 4 + (row >> 6)
        out_ref[half] = nt_dot(inverse, (column == radius).astype(BF)).astype(BF)
    valid = jnp.where(assign_ref[...] <= place_ref[1], 1.0, 0.0)
    doubled = (row == (column >> 1)).astype(BF)
    valid_ref[...] = jnp.dot(
        jnp.broadcast_to(valid, (8, 256)).astype(BF), doubled, preferred_element_type=F32
    )


def solve_kernel(valid_ref, inverse_ref, right_ref, out_ref):
    right = right_ref[...].reshape(1024, 256)
    solved = nt_dot(inverse_ref[0], right[:512]) + nt_dot(inverse_ref[1], right[512:])
    out_ref[...] = (solved * (valid_ref[0:1, :] * 0.5)).astype(BF)


VMEM = pl.BlockSpec(memory_space=pltpu.VMEM)
SMEM = pl.BlockSpec(memory_space=pltpu.SMEM)
HBM = pl.BlockSpec(memory_space=pltpu.HBM)


def call(kernel, out, ins, scratch=(), flops=0, vmem=24, outs=None):
    return pl.pallas_call(
        kernel,
        out_shape=out,
        in_specs=ins,
        out_specs=outs or jax.tree.map(lambda _: VMEM, out),
        scratch_shapes=list(scratch),
        compiler_params=pltpu.CompilerParams(vmem_limit_bytes=vmem * 1024 * 1024),
        cost_estimate=pl.CostEstimate(flops=flops, bytes_accessed=2 * 1024 * 1024, transcendentals=0),
    )


def bf16(*shape):
    return jax.ShapeDtypeStruct(shape, BF)


def shards(forcing, legendre, assign, inverse, previous):
    x, core, rad = lax.axis_index("x"), lax.axis_index("core"), lax.axis_index(RAD)
    orders = assign.reshape(1, 256)
    place = jnp.stack([rad * 4 + x, (x * 2 + core) * 64 + rad, x]).astype(jnp.int32)

    sent = call(
        fourier_kernel,
        bf16(512, 2, 640),
        [VMEM, HBM, HBM],
        [
            pltpu.VMEM((8, 96, LON), BF),
            pltpu.VMEM((8, 64, 512), BF),
            pltpu.VMEM((512, LON), BF),
            pltpu.VMEM((512, 2, 640), BF),
            pltpu.SemaphoreType.DMA((2,)),
            pltpu.SemaphoreType.DMA((4,)),
        ],
        2 * 512 * 768 * 1024,
        60,
        HBM,
    )(orders, forcing, previous)
    sent, legendre = lax.optimization_barrier((sent, legendre))
    arrived = lax.all_to_all(sent, ("core", "x") + RAD, 0, 0, tiled=True)

    by_order = legendre.transpose(0, 2, 1)
    pieces = [lax.dynamic_index_in_dim(by_order, x, 0, keepdims=False)]
    for shift in range(1, 4):
        mine = lax.dynamic_index_in_dim(by_order, (x + shift) % 4, 0, keepdims=False)
        pieces.append(lax.ppermute(mine, "x", [(i, (i + shift) % 4) for i in range(4)]))
    whole = lax.all_gather(jnp.stack(pieces), "core", axis=0)
    weights, parted = call(
        legendre_kernel, (bf16(512, 1280), bf16(512, 512)), [VMEM, SMEM, VMEM], (), 2 * 512 * 512 * 768
    )(orders, place, whole)
    solver, valid = call(
        inverse_kernel,
        (bf16(2, 512, 256), jax.ShapeDtypeStruct((8, 512), F32)),
        [VMEM, SMEM, VMEM],
        (),
        2 * 512**3,
    )(orders, place, inverse)

    right = call(
        spectrum_kernel,
        bf16(512, 2, 256),
        [VMEM] * 3,
        [pltpu.VMEM((1024, 640), BF), pltpu.VMEM((512, 1280), BF)],
        2 * 512 * 512 * 1792,
    )(arrived, weights, parted)
    right = lax.all_to_all(right, ("core",) + RAD + ("x",), 0, 0, tiled=True)
    solved = call(solve_kernel, bf16(512, 512), [VMEM] * 3, (), 2 * 512**3)(valid, solver, right)
    out = lax.all_to_all(solved.reshape(64, 8, 512), RAD, 0, 0, tiled=True)
    return out.transpose(1, 0, 2)


def solution(mesh):
    split = Mesh(mesh.devices.reshape(4, 2, 8, 8), LAT + RAD)
    placed = (
        P(RAD, LAT, None),
        P(RAD, None, LAT),
        P(),
        P(LAT + RAD, None, None),
        P(RAD, LAT, None),
    )
    return jax.shard_map(shards, mesh=split, in_specs=placed, out_specs=P(RAD, LAT, None), check_vma=False)
```

```python
import math

import jax
import jax.numpy as jnp
from jax import lax
from jax.experimental import pallas as pl
from jax.experimental.pallas import tpu as pltpu
from jax.sharding import Mesh, PartitionSpec as P

NR = 512
L = 512
LON = 1024
BF = jnp.bfloat16
F32 = jnp.float32
RAD = ("zh", "zl", "y")
LAT = ("x", "core")


def nt_dot(a, b):
    return lax.dot_general(a, b, (((1,), (1,)), ((), ())), preferred_element_type=F32)


def iota(shape, dim):
    return lax.broadcasted_iota(jnp.int32, shape, dim)


def cos_sin(phase):
    quadrant = ((phase + 128) >> 8) & 3
    rest = ((phase + 128) & 255) - 128
    x = rest.astype(F32) * (2.0 * math.pi / LON)
    x2 = x * x
    sin_x = x * (1.0 + x2 * (-1.0 / 6 + x2 * (1.0 / 120 + x2 * (-1.0 / 5040 + x2 * (1.0 / 362880)))))
    cos_x = 1.0 + x2 * (-0.5 + x2 * (1.0 / 24 + x2 * (-1.0 / 720 + x2 * (1.0 / 40320))))
    swap = (quadrant & 1) == 1
    cos_part = jnp.where(swap, sin_x, cos_x)
    sin_part = jnp.where(swap, cos_x, sin_x)
    cos_sign = jnp.where((quadrant == 1) | (quadrant == 2), -1.0, 1.0)
    sin_sign = jnp.where(quadrant >= 2, -1.0, 1.0)
    return cos_part * cos_sign, sin_part * sin_sign


def fourier_kernel(
    assign_ref, forcing_hbm, previous_hbm, out_hbm, forcing_ref, previous_ref, table_ref, out_ref, in_sems, out_sems
):
    previous_copy = pltpu.make_async_copy(previous_hbm, previous_ref, in_sems.at[1])
    previous_copy.start()
    forcing_copy = pltpu.make_async_copy(forcing_hbm, forcing_ref, in_sems.at[0])
    forcing_copy.start()
    row = iota((512, 1), 0)
    slot = ((row >> 4) & 3) * 64 + (row >> 8) * 32 + ((row >> 1) & 7) * 4 + ((row >> 6) & 3)
    orders = jnp.sum(jnp.where(iota((512, 256), 1) == slot, assign_ref[...], 0), axis=1, keepdims=True)
    lane = iota((512, 128), 1)
    cos_now, sin_now = cos_sin((orders * lane + (row & 1) * (LON // 4)) & (LON - 1))
    cos_half, sin_half = cos_now[:, 64:65], sin_now[:, 64:65]
    sign = (1 - 2 * (row & 1)).astype(F32)
    cos_step = jnp.broadcast_to(sign * (1.0 - 2.0 * sin_half * sin_half), (512, 128))
    sin_step = jnp.broadcast_to(sign * (2.0 * sin_half * cos_half), (512, 128))
    cos_now, sin_now = cos_now * LON**-0.5, sin_now * LON**-0.5
    for q in range(LON // 128):
        table_ref[:, q * 128 : q * 128 + 128] = cos_now.astype(BF)
        cos_now, sin_now = cos_now * cos_step - sin_now * sin_step, sin_now * cos_step + cos_now * sin_step
    table = table_ref[...]
    reorder = (iota((512, 512), 1) == slot * 2 + (row & 1)).astype(BF)
    previous_copy.wait()
    previous = previous_ref[...].reshape(512, 512)
    forcing_copy.wait()
    out_copies = []
    for block in range(2):
        rows = slice(block * 256, block * 256 + 256)
        dests = pl.ds(block * 128, 128)
        for h in range(3):
            part = forcing_ref[:, h * 32 : h * 32 + 32, :].reshape(256, LON)
            part = nt_dot(table[rows], part).astype(BF)
            out_ref[dests, :, h * 256 : h * 256 + 256] = part.reshape(128, 2, 256)
        out_ref[dests, :, 768:1280] = nt_dot(reorder[rows], previous).astype(BF).reshape(128, 2, 512)
        copy = pltpu.make_async_copy(out_ref.at[dests], out_hbm.at[dests], out_sems.at[block])
        copy.start()
        out_copies.append(copy)
    for copy in out_copies:
        copy.wait()


def legendre_kernel(assign_ref, place_ref, legendre_ref, out_ref, parted_ref):
    order = jnp.sum(jnp.where(iota((1, 256), 1) == place_ref[0], assign_ref[...], 0), axis=1, keepdims=True)
    row = iota((512, 1), 0)
    core, x = (row >> 5) & 1, row & 3
    inner = ((row >> 6) & 3) * 16 + (row >> 8) * 8 + ((row >> 2) & 7)
    degree = (2 * x + core) * 64 + inner
    column = iota((512, 512), 1)
    kept = jnp.where((column == degree) & (degree >= order), 1.0, 0.0).astype(BF)
    x_here, zl = place_ref[2], place_ref[3]
    for h in range(3):
        rows = pl.ds(h * 32, 32)
        for core_from in range(2):
            cross = (zl + core_from) & 1
            pieces = [
                legendre_ref[((x_here - x_from) & 3) * 2 + cross, rows, :] for x_from in range(4)
            ]
            at = h * 256 + core_from * 128
            out_ref[:, at : at + 128] = nt_dot(kept, jnp.concatenate(pieces, axis=0)).astype(BF)
    out_ref[:, 768:1280] = jnp.where(column == core * 256 + x * 64 + inner, 2.0, 0.0).astype(BF)
    parted_ref[...] = (column == (row & 1) * 256 + (row >> 1)).astype(BF)


def roll(a, shift):
    return pltpu.roll(a, shift, 1)


def spectrum_kernel(arrived_ref, weights_ref, parted_ref, out_ref, rows_ref, gathered_ref):
    rows_ref[...] = arrived_ref[...].reshape(512, 1280)
    lane = iota((64, 128), 1)
    low_half = lane < 64
    even_quarter = (lane & 32) == 0

    def tile(block, at):
        return rows_ref[block * 64 : block * 64 + 64, at : at + 128].astype(F32)

    def place(rho, at, value):
        gathered_ref[rho * 64 : rho * 64 + 64, at : at + 128] = value.astype(BF)

    for h in range(3):
        for high in range(2):
            for core in range(2):
                a = [tile(core * 4 + x, h * 256 + high * 128) for x in range(4)]
                b0 = jnp.where(low_half, a[0], roll(a[2], 64))
                b2 = jnp.where(low_half, roll(a[0], 64), a[2])
                b1 = jnp.where(low_half, a[1], roll(a[3], 64))
                b3 = jnp.where(low_half, roll(a[1], 64), a[3])
                at, rho = h * 256 + core * 128, high * 4
                place(rho, at, jnp.where(even_quarter, b0, roll(b1, 32)))
                place(rho + 1, at, jnp.where(even_quarter, roll(b0, 96), b1))
                place(rho + 2, at, jnp.where(even_quarter, b2, roll(b3, 32)))
                place(rho + 3, at, jnp.where(even_quarter, roll(b2, 96), b3))
    for pair in range(4):
        for two in range(4):
            at = 768 + pair * 128
            a0, a1 = tile(two * 2, at), tile(two * 2 + 1, at)
            to = 768 + two * 128
            place(pair * 2, to, jnp.where(low_half, a0, roll(a1, 64)))
            place(pair * 2 + 1, to, jnp.where(low_half, roll(a0, 64), a1))
    right = nt_dot(weights_ref[...], gathered_ref[...]).astype(BF)
    right = jnp.dot(right, parted_ref[...], preferred_element_type=F32).astype(BF)
    out_ref[...] = right.reshape(512, 2, 256)


def inverse_kernel(assign_ref, place_ref, inverse_ref, out_ref, valid_ref):
    inverse = inverse_ref[0].astype(BF)
    row, column = iota((256, 512), 0), iota((256, 512), 1)
    for zl in range(2):
        radius = ((row >> 3) & 3) * 128 + zl * 64 + (row & 7) * 8 + (row >> 5)
        out_ref[zl] = nt_dot(inverse, (column == radius).astype(BF)).astype(BF)
    valid = jnp.where(assign_ref[...] <= place_ref[1], 1.0, 0.0)
    doubled = (row == (column >> 1)).astype(BF)
    valid_ref[...] = jnp.dot(
        jnp.broadcast_to(valid, (8, 256)).astype(BF), doubled, preferred_element_type=F32
    )


def solve_kernel(valid_ref, inverse_ref, right_ref, out_ref):
    right = right_ref[...].reshape(1024, 256)
    solved = nt_dot(inverse_ref[0], right[:512]) + nt_dot(inverse_ref[1], right[512:])
    out_ref[...] = (solved * (valid_ref[0:1, :] * 0.5)).astype(BF)


VMEM = pl.BlockSpec(memory_space=pltpu.VMEM)
SMEM = pl.BlockSpec(memory_space=pltpu.SMEM)
HBM = pl.BlockSpec(memory_space=pltpu.HBM)


def call(kernel, out, ins, scratch=(), flops=0, vmem=24, outs=None):
    return pl.pallas_call(
        kernel,
        out_shape=out,
        in_specs=ins,
        out_specs=outs or jax.tree.map(lambda _: VMEM, out),
        scratch_shapes=list(scratch),
        compiler_params=pltpu.CompilerParams(vmem_limit_bytes=vmem * 1024 * 1024),
        cost_estimate=pl.CostEstimate(flops=flops, bytes_accessed=2 * 1024 * 1024, transcendentals=0),
    )


def bf16(*shape):
    return jax.ShapeDtypeStruct(shape, BF)


def shards(forcing, legendre, assign, inverse, previous):
    x, core = lax.axis_index("x"), lax.axis_index("core")
    zh, zl, y = lax.axis_index("zh"), lax.axis_index("zl"), lax.axis_index("y")
    orders = assign.reshape(1, 256)
    slot = zh * 64 + core * 32 + y * 4 + x
    degree = (x * 2 + core) * 64 + zh * 16 + zl * 8 + y
    place = jnp.stack([slot, degree, x, zl]).astype(jnp.int32)

    sent = call(
        fourier_kernel,
        bf16(256, 2, 1280),
        [VMEM, HBM, HBM],
        [
            pltpu.VMEM((8, 96, LON), BF),
            pltpu.VMEM((8, 64, 512), BF),
            pltpu.VMEM((512, LON), BF),
            pltpu.VMEM((256, 2, 1280), BF),
            pltpu.SemaphoreType.DMA((2,)),
            pltpu.SemaphoreType.DMA((2,)),
        ],
        2 * 512 * 768 * 1024,
        60,
        HBM,
    )(orders, forcing, previous)
    sent, legendre = lax.optimization_barrier((sent, legendre))
    arrived = lax.all_to_all(sent, ("core", "x", "zh", "y"), 0, 0, tiled=True)

    by_order = legendre.transpose(0, 2, 1)
    pieces = []
    for shift in range(4):
        mine = lax.dynamic_index_in_dim(by_order, (x + shift) % 4, 0, keepdims=False)
        for cross in range(2):
            pairs = [
                (i, (i // 4 + shift) % 4 * 4 + i % 2 * 2 + (i // 2 % 2 ^ cross)) for i in range(16)
            ]
            pieces.append(lax.ppermute(mine, ("x", "core", "zl"), pairs))
    whole = jnp.stack(pieces)
    weights, parted = call(
        legendre_kernel, (bf16(512, 1280), bf16(512, 512)), [VMEM, SMEM, VMEM], (), 2 * 512 * 512 * 768
    )(orders, place, whole)
    solver, valid = call(
        inverse_kernel,
        (bf16(2, 512, 256), jax.ShapeDtypeStruct((8, 512), F32)),
        [VMEM, SMEM, VMEM],
        (),
        2 * 512**3,
    )(orders, place, inverse)

    right = call(
        spectrum_kernel,
        bf16(512, 2, 256),
        [VMEM] * 3,
        [pltpu.VMEM((512, 1280), BF)] * 2,
        2 * 512 * 512 * 1792,
    )(arrived, weights, parted)
    right = lax.all_to_all(right, ("zl", "zh", "core", "y", "x"), 0, 0, tiled=True)
    solved = call(solve_kernel, bf16(512, 512), [VMEM] * 3, (), 2 * 512**3)(valid, solver, right)
    out = lax.all_to_all(solved.reshape(64, 8, 512), RAD, 0, 0, tiled=True)
    return out.transpose(1, 0, 2)


def solution(mesh):
    split = Mesh(mesh.devices.reshape(4, 2, 4, 2, 8), LAT + RAD)
    placed = (
        P(RAD, LAT, None),
        P(RAD, None, LAT),
        P(),
        P(LAT + RAD, None, None),
        P(RAD, LAT, None),
    )
    return jax.shard_map(shards, mesh=split, in_specs=placed, out_specs=P(RAD, LAT, None), check_vma=False)
```

```python
import math

import jax
import jax.numpy as jnp
from jax import lax
from jax.experimental import pallas as pl
from jax.experimental.pallas import tpu as pltpu
from jax.sharding import Mesh, PartitionSpec as P

NR = 512
L = 512
LON = 1024
BF = jnp.bfloat16
F32 = jnp.float32
RAD = ("z", "y")
LAT = ("x", "core")


def nt_dot(a, b):
    return lax.dot_general(a, b, (((1,), (1,)), ((), ())), preferred_element_type=F32)


def iota(shape, dim):
    return lax.broadcasted_iota(jnp.int32, shape, dim)


def cos_sin(phase):
    quadrant = ((phase + 128) >> 8) & 3
    rest = ((phase + 128) & 255) - 128
    x = rest.astype(F32) * (2.0 * math.pi / LON)
    x2 = x * x
    sin_x = x * (1.0 + x2 * (-1.0 / 6 + x2 * (1.0 / 120 + x2 * (-1.0 / 5040 + x2 * (1.0 / 362880)))))
    cos_x = 1.0 + x2 * (-0.5 + x2 * (1.0 / 24 + x2 * (-1.0 / 720 + x2 * (1.0 / 40320))))
    swap = (quadrant & 1) == 1
    cos_part = jnp.where(swap, sin_x, cos_x)
    sin_part = jnp.where(swap, cos_x, sin_x)
    cos_sign = jnp.where((quadrant == 1) | (quadrant == 2), -1.0, 1.0)
    sin_sign = jnp.where(quadrant >= 2, -1.0, 1.0)
    return cos_part * cos_sign, sin_part * sin_sign


def fourier_kernel(
    assign_ref, forcing_hbm, previous_hbm, out_hbm, forcing_ref, previous_ref, table_ref, out_ref, in_sems, out_sems
):
    previous_copy = pltpu.make_async_copy(previous_hbm, previous_ref, in_sems.at[1])
    previous_copy.start()
    forcing_copy = pltpu.make_async_copy(forcing_hbm, forcing_ref, in_sems.at[0])
    forcing_copy.start()
    row = iota((512, 1), 0)
    slot = ((row >> 1) & 63) * 4 + (row >> 7)
    orders = jnp.sum(jnp.where(iota((512, 256), 1) == slot, assign_ref[...], 0), axis=1, keepdims=True)
    lane = iota((512, 128), 1)
    cos_now, sin_now = cos_sin((orders * lane + (row & 1) * (LON // 4)) & (LON - 1))
    cos_half, sin_half = cos_now[:, 64:65], sin_now[:, 64:65]
    sign = (1 - 2 * (row & 1)).astype(F32)
    cos_step = jnp.broadcast_to(sign * (1.0 - 2.0 * sin_half * sin_half), (512, 128))
    sin_step = jnp.broadcast_to(sign * (2.0 * sin_half * cos_half), (512, 128))
    cos_now, sin_now = cos_now * LON**-0.5, sin_now * LON**-0.5
    for q in range(LON // 128):
        table_ref[:, q * 128 : q * 128 + 128] = cos_now.astype(BF)
        cos_now, sin_now = cos_now * cos_step - sin_now * sin_step, sin_now * cos_step + cos_now * sin_step
    table = table_ref[...]
    reorder = (iota((512, 512), 1) == slot * 2 + (row & 1)).astype(BF)
    previous_copy.wait()
    previous = previous_ref[...].reshape(512, 512)
    forcing_copy.wait()
    out_copies = []
    for block in range(2):
        rows = slice(block * 256, block * 256 + 256)
        parts = []
        for h in range(3):
            part = forcing_ref[:, h * 32 : h * 32 + 32, :].reshape(256, LON)
            parts.append(nt_dot(table[rows], part).astype(BF))
        parts.append(nt_dot(reorder[rows], previous).astype(BF))
        dests = pl.ds(block * 128, 128)
        out_ref[dests] = jnp.concatenate(parts, axis=1).reshape(128, 2, 1280)
        copy = pltpu.make_async_copy(out_ref.at[dests], out_hbm.at[dests], out_sems.at[block])
        copy.start()
        out_copies.append(copy)
    for copy in out_copies:
        copy.wait()


def legendre_kernel(assign_ref, place_ref, legendre_ref, own_ref, other_ref):
    order = jnp.sum(jnp.where(iota((1, 256), 1) == place_ref[0], assign_ref[...], 0), axis=1, keepdims=True)
    x_here, core = place_ref[2], place_ref[3]
    row, column = iota((256, 1), 0), iota((256, 512), 1)
    x, rad = row & 3, row >> 2
    kept = []
    for of_core in (core, 1 - core):
        degree = (2 * x + of_core) * 64 + rad
        kept.append(jnp.where((column == degree) & (degree >= order), 1.0, 0.0).astype(BF))
    for h in range(3):
        pieces = [legendre_ref[(x_here - x_from) & 3, h * 32 : h * 32 + 32, :] for x_from in range(4)]
        pieces = jnp.concatenate(pieces, axis=0)
        own_ref[:, h * 128 : h * 128 + 128] = nt_dot(kept[0], pieces).astype(BF)
        other_ref[:, h * 128 : h * 128 + 128] = nt_dot(kept[1], pieces).astype(BF)
    own_ref[:, 384:640] = jnp.where(iota((256, 256), 1) == x * 64 + rad, 2.0, 0.0).astype(BF)


def roll(a, shift):
    return pltpu.roll(a, shift, 1)


def spectrum_kernel(arrived_ref, weights_ref, gathered_ref, out_ref, rows_ref):
    rows_ref[...] = arrived_ref[...].reshape(512, 1280)
    lane = iota((128, 128), 1)
    low_half = lane < 64
    even_quarter = (lane & 32) == 0

    def tile(block, at):
        return rows_ref[block * 128 : block * 128 + 128, at : at + 128].astype(F32)

    def place(rho, at, value):
        gathered_ref[rho * 128 : rho * 128 + 128, at : at + 128] = value.astype(BF)

    for h in range(3):
        for high in range(2):
            a = [tile(x, h * 256 + high * 128) for x in range(4)]
            b0 = jnp.where(low_half, a[0], roll(a[2], 64))
            b2 = jnp.where(low_half, roll(a[0], 64), a[2])
            b1 = jnp.where(low_half, a[1], roll(a[3], 64))
            b3 = jnp.where(low_half, roll(a[1], 64), a[3])
            at, rho = h * 128, high * 4
            place(rho, at, jnp.where(even_quarter, b0, roll(b1, 32)))
            place(rho + 1, at, jnp.where(even_quarter, roll(b0, 96), b1))
            place(rho + 2, at, jnp.where(even_quarter, b2, roll(b3, 32)))
            place(rho + 3, at, jnp.where(even_quarter, roll(b2, 96), b3))
    out_ref[...] = nt_dot(weights_ref[...], gathered_ref[:, :384]).astype(BF)
    for pair in range(4):
        for two in range(2):
            at = 768 + pair * 128
            a0, a1 = tile(two * 2, at), tile(two * 2 + 1, at)
            to = 384 + two * 128
            place(pair * 2, to, jnp.where(low_half, a0, roll(a1, 64)))
            place(pair * 2 + 1, to, jnp.where(low_half, roll(a0, 64), a1))


def own_kernel(gathered_ref, weights_ref, out_ref):
    out_ref[...] = nt_dot(weights_ref[...], gathered_ref[...])


def right_kernel(own_ref, received_ref, out_ref):
    right = (own_ref[...] + received_ref[...].astype(F32)).astype(BF)
    row, column = iota((256, 256), 0), iota((256, 256), 1)
    parted = (column == (row & 1) * 128 + (row >> 1)).astype(BF)
    parts = []
    for i in range(4):
        part = right[:, i * 256 : i * 256 + 256]
        parts.append(jnp.dot(part, parted, preferred_element_type=F32).astype(BF))
    parts = [part[:, :128] for part in parts] + [part[:, 128:] for part in parts]
    out_ref[...] = jnp.concatenate(parts, axis=1).reshape(256, 2, 512)


def inverse_kernel(assign_ref, place_ref, inverse_ref, out_ref, valid_ref):
    row, column = iota((512, 1), 0), iota((512, 512), 1)
    regroup = (column == (row & 63) * 8 + (row >> 6)).astype(BF)
    out_ref[...] = nt_dot(inverse_ref[0].astype(BF), regroup).astype(BF)
    valid = jnp.where(assign_ref[...] <= place_ref[1], 1.0, 0.0)
    row, column = iota((256, 512), 0), iota((256, 512), 1)
    doubled = (row == (column >> 1)).astype(BF)
    valid_ref[...] = jnp.dot(
        jnp.broadcast_to(valid, (8, 256)).astype(BF), doubled, preferred_element_type=F32
    )


def solve_kernel(valid_ref, inverse_ref, right_ref, out_ref):
    solved = nt_dot(inverse_ref[...], right_ref[...].reshape(512, 512))
    out_ref[...] = (solved * (valid_ref[0:1, :] * 0.5)).astype(BF)


VMEM = pl.BlockSpec(memory_space=pltpu.VMEM)
SMEM = pl.BlockSpec(memory_space=pltpu.SMEM)
HBM = pl.BlockSpec(memory_space=pltpu.HBM)


def call(kernel, out, ins, scratch=(), flops=0, vmem=24, outs=None):
    return pl.pallas_call(
        kernel,
        out_shape=out,
        in_specs=ins,
        out_specs=outs or jax.tree.map(lambda _: VMEM, out),
        scratch_shapes=list(scratch),
        compiler_params=pltpu.CompilerParams(vmem_limit_bytes=vmem * 1024 * 1024),
        cost_estimate=pl.CostEstimate(flops=flops, bytes_accessed=2 * 1024 * 1024, transcendentals=0),
    )


def bf16(*shape):
    return jax.ShapeDtypeStruct(shape, BF)


def shards(forcing, legendre, assign, inverse, previous):
    x, core, rad = lax.axis_index("x"), lax.axis_index("core"), lax.axis_index(RAD)
    orders = assign.reshape(1, 256)
    place = jnp.stack([rad * 4 + x, (x * 2 + core) * 64 + rad, x, core]).astype(jnp.int32)

    sent = call(
        fourier_kernel,
        bf16(256, 2, 1280),
        [VMEM, HBM, HBM],
        [
            pltpu.VMEM((8, 96, LON), BF),
            pltpu.VMEM((8, 64, 512), BF),
            pltpu.VMEM((512, LON), BF),
            pltpu.VMEM((256, 2, 1280), BF),
            pltpu.SemaphoreType.DMA((2,)),
            pltpu.SemaphoreType.DMA((2,)),
        ],
        2 * 512 * 768 * 1024,
        60,
        HBM,
    )(orders, forcing, previous)
    sent, legendre = lax.optimization_barrier((sent, legendre))
    arrived = lax.all_to_all(sent, ("x",) + RAD, 0, 0, tiled=True)

    by_order = legendre.transpose(0, 2, 1)
    pieces = [lax.dynamic_index_in_dim(by_order, x, 0, keepdims=False)]
    for shift in range(1, 4):
        mine = lax.dynamic_index_in_dim(by_order, (x + shift) % 4, 0, keepdims=False)
        pieces.append(lax.ppermute(mine, "x", [(i, (i + shift) % 4) for i in range(4)]))
    own_weights, other_weights = call(
        legendre_kernel, (bf16(256, 640), bf16(256, 384)), [VMEM, SMEM, VMEM], (), 2 * 512 * 512 * 384
    )(orders, place, jnp.stack(pieces))
    solver, valid = call(
        inverse_kernel,
        (bf16(512, 512), jax.ShapeDtypeStruct((8, 512), F32)),
        [VMEM, SMEM, VMEM],
        (),
        2 * 512**3,
    )(orders, place, inverse)

    gathered, other = call(
        spectrum_kernel,
        (bf16(1024, 640), bf16(256, 1024)),
        [VMEM] * 2,
        [pltpu.VMEM((512, 1280), BF)],
        2 * 256 * 384 * 1024,
    )(arrived, other_weights)
    received = lax.ppermute(other, "core", [(0, 1), (1, 0)])
    own = call(own_kernel, jax.ShapeDtypeStruct((256, 1024), F32), [VMEM] * 2, (), 2 * 256 * 640 * 1024)(
        gathered, own_weights
    )
    right = call(right_kernel, bf16(256, 2, 512), [VMEM] * 2, (), 2 * 256 * 256 * 1024)(own, received)
    right = lax.all_to_all(right, RAD + ("x",), 0, 0, tiled=True)
    solved = call(solve_kernel, bf16(512, 512), [VMEM] * 3, (), 2 * 512**3)(valid, solver, right)
    out = lax.all_to_all(solved.reshape(64, 8, 512), RAD, 0, 0, tiled=True)
    return out.transpose(1, 0, 2)


def solution(mesh):
    split = Mesh(mesh.devices.reshape(4, 2, 8, 8), LAT + RAD)
    placed = (
        P(RAD, LAT, None),
        P(RAD, None, LAT),
        P(),
        P(LAT + RAD, None, None),
        P(RAD, LAT, None),
    )
    return jax.shard_map(shards, mesh=split, in_specs=placed, out_specs=P(RAD, LAT, None), check_vma=False)
```

```python
import math

import jax
import jax.numpy as jnp
from jax import lax
from jax.experimental import pallas as pl
from jax.experimental.pallas import tpu as pltpu
from jax.sharding import Mesh, PartitionSpec as P

NR = 512
L = 512
LON = 1024
BF = jnp.bfloat16
F32 = jnp.float32
RAD = ("z", "y")
LAT = ("x", "core")


def nt_dot(a, b):
    return lax.dot_general(a, b, (((1,), (1,)), ((), ())), preferred_element_type=F32)


def iota(shape, dim):
    return lax.broadcasted_iota(jnp.int32, shape, dim)


def cos_sin(phase):
    quadrant = ((phase + 128) >> 8) & 3
    rest = ((phase + 128) & 255) - 128
    x = rest.astype(F32) * (2.0 * math.pi / LON)
    x2 = x * x
    sin_x = x * (1.0 + x2 * (-1.0 / 6 + x2 * (1.0 / 120 + x2 * (-1.0 / 5040 + x2 * (1.0 / 362880)))))
    cos_x = 1.0 + x2 * (-0.5 + x2 * (1.0 / 24 + x2 * (-1.0 / 720 + x2 * (1.0 / 40320))))
    swap = (quadrant & 1) == 1
    cos_part = jnp.where(swap, sin_x, cos_x)
    sin_part = jnp.where(swap, cos_x, sin_x)
    cos_sign = jnp.where((quadrant == 1) | (quadrant == 2), -1.0, 1.0)
    sin_sign = jnp.where(quadrant >= 2, -1.0, 1.0)
    return cos_part * cos_sign, sin_part * sin_sign


def fourier_kernel(
    assign_ref, forcing_hbm, previous_hbm, out_hbm, forcing_ref, previous_ref, table_ref, out_ref, in_sems, out_sems
):
    previous_copy = pltpu.make_async_copy(previous_hbm, previous_ref, in_sems.at[1])
    previous_copy.start()
    forcing_copy = pltpu.make_async_copy(forcing_hbm, forcing_ref, in_sems.at[0])
    forcing_copy.start()
    row = iota((512, 1), 0)
    slot = ((row >> 1) & 63) * 4 + (row >> 7)
    orders = jnp.sum(jnp.where(iota((512, 256), 1) == slot, assign_ref[...], 0), axis=1, keepdims=True)
    lane = iota((512, 128), 1)
    cos_now, sin_now = cos_sin((orders * lane + (row & 1) * (LON // 4)) & (LON - 1))
    cos_half, sin_half = cos_now[:, 64:65], sin_now[:, 64:65]
    sign = (1 - 2 * (row & 1)).astype(F32)
    cos_step = jnp.broadcast_to(sign * (1.0 - 2.0 * sin_half * sin_half), (512, 128))
    sin_step = jnp.broadcast_to(sign * (2.0 * sin_half * cos_half), (512, 128))
    cos_now, sin_now = cos_now * LON**-0.5, sin_now * LON**-0.5
    for q in range(LON // 128):
        table_ref[:, q * 128 : q * 128 + 128] = cos_now.astype(BF)
        cos_now, sin_now = cos_now * cos_step - sin_now * sin_step, sin_now * cos_step + cos_now * sin_step
    table = table_ref[...]
    reorder = (iota((512, 512), 1) == slot * 2 + (row & 1)).astype(BF)
    previous_copy.wait()
    previous = previous_ref[...].reshape(512, 512)
    forcing_copy.wait()
    out_copies = []
    for block in range(2):
        rows = slice(block * 256, block * 256 + 256)
        parts = []
        for h in range(3):
            part = forcing_ref[:, h * 32 : h * 32 + 32, :].reshape(256, LON)
            parts.append(nt_dot(table[rows], part).astype(BF))
        parts.append(nt_dot(reorder[rows], previous).astype(BF))
        dests = pl.ds(block * 128, 128)
        out_ref[dests] = jnp.concatenate(parts, axis=1).reshape(128, 2, 1280)
        copy = pltpu.make_async_copy(out_ref.at[dests], out_hbm.at[dests], out_sems.at[block])
        copy.start()
        out_copies.append(copy)
    for copy in out_copies:
        copy.wait()


def legendre_kernel(assign_ref, place_ref, legendre_ref, own_ref, other_ref):
    order = jnp.sum(jnp.where(iota((1, 256), 1) == place_ref[0], assign_ref[...], 0), axis=1, keepdims=True)
    x_here, core = place_ref[2], place_ref[3]
    row, column = iota((256, 1), 0), iota((256, 512), 1)
    x, rad = row & 3, row >> 2
    kept = []
    for of_core in (core, 1 - core):
        degree = (2 * x + of_core) * 64 + rad
        kept.append(jnp.where((column == degree) & (degree >= order), 1.0, 0.0).astype(BF))
    for h in range(3):
        pieces = [legendre_ref[(x_here - x_from) & 3, h * 32 : h * 32 + 32, :] for x_from in range(4)]
        pieces = jnp.concatenate(pieces, axis=0)
        own_ref[:, h * 128 : h * 128 + 128] = nt_dot(kept[0], pieces).astype(BF)
        other_ref[:, h * 128 : h * 128 + 128] = nt_dot(kept[1], pieces).astype(BF)
    own_ref[:, 384:640] = jnp.where(iota((256, 256), 1) == x * 64 + rad, 2.0, 0.0).astype(BF)


def roll(a, shift):
    return pltpu.roll(a, shift, 1)


def spectrum_kernel(arrived_ref, weights_ref, gathered_ref, out_ref, rows_ref):
    rows_ref[...] = arrived_ref[...].reshape(512, 1280)
    lane = iota((128, 128), 1)
    low_half = lane < 64
    even_quarter = (lane & 32) == 0

    def tile(block, at):
        return rows_ref[block * 128 : block * 128 + 128, at : at + 128].astype(F32)

    def place(rho, at, value):
        gathered_ref[rho * 128 : rho * 128 + 128, at : at + 128] = value.astype(BF)

    for h in range(3):
        for high in range(2):
            a = [tile(x, h * 256 + high * 128) for x in range(4)]
            b0 = jnp.where(low_half, a[0], roll(a[2], 64))
            b2 = jnp.where(low_half, roll(a[0], 64), a[2])
            b1 = jnp.where(low_half, a[1], roll(a[3], 64))
            b3 = jnp.where(low_half, roll(a[1], 64), a[3])
            at, rho = h * 128, high * 4
            place(rho, at, jnp.where(even_quarter, b0, roll(b1, 32)))
            place(rho + 1, at, jnp.where(even_quarter, roll(b0, 96), b1))
            place(rho + 2, at, jnp.where(even_quarter, b2, roll(b3, 32)))
            place(rho + 3, at, jnp.where(even_quarter, roll(b2, 96), b3))
    out_ref[...] = nt_dot(weights_ref[...], gathered_ref[:, :384]).astype(BF)
    for pair in range(4):
        for two in range(2):
            at = 768 + pair * 128
            a0, a1 = tile(two * 2, at), tile(two * 2 + 1, at)
            to = 384 + two * 128
            place(pair * 2, to, jnp.where(low_half, a0, roll(a1, 64)))
            place(pair * 2 + 1, to, jnp.where(low_half, roll(a0, 64), a1))


def right_kernel(place_ref, gathered_ref, weights_ref, received_ref, out_ref):
    own = nt_dot(weights_ref[...], gathered_ref[...])
    right = (own + received_ref[1 - place_ref[3]].astype(F32)).astype(BF)
    row, column = iota((256, 256), 0), iota((256, 256), 1)
    parted = (column == (row & 1) * 128 + (row >> 1)).astype(BF)
    parts = []
    for i in range(4):
        part = right[:, i * 256 : i * 256 + 256]
        parts.append(jnp.dot(part, parted, preferred_element_type=F32).astype(BF))
    parts = [part[:, :128] for part in parts] + [part[:, 128:] for part in parts]
    out_ref[...] = jnp.concatenate(parts, axis=1).reshape(256, 2, 512)


def inverse_kernel(assign_ref, place_ref, inverse_ref, out_ref, valid_ref):
    row, column = iota((512, 1), 0), iota((512, 512), 1)
    regroup = (column == (row & 63) * 8 + (row >> 6)).astype(BF)
    out_ref[...] = nt_dot(inverse_ref[0].astype(BF), regroup).astype(BF)
    valid = jnp.where(assign_ref[...] <= place_ref[1], 1.0, 0.0)
    row, column = iota((256, 512), 0), iota((256, 512), 1)
    doubled = (row == (column >> 1)).astype(BF)
    valid_ref[...] = jnp.dot(
        jnp.broadcast_to(valid, (8, 256)).astype(BF), doubled, preferred_element_type=F32
    )


def solve_kernel(valid_ref, inverse_ref, right_ref, out_ref):
    solved = nt_dot(inverse_ref[...], right_ref[...].reshape(512, 512))
    out_ref[...] = (solved * (valid_ref[0:1, :] * 0.5)).astype(BF)


VMEM = pl.BlockSpec(memory_space=pltpu.VMEM)
SMEM = pl.BlockSpec(memory_space=pltpu.SMEM)
HBM = pl.BlockSpec(memory_space=pltpu.HBM)


def call(kernel, out, ins, scratch=(), flops=0, vmem=24, outs=None):
    return pl.pallas_call(
        kernel,
        out_shape=out,
        in_specs=ins,
        out_specs=outs or jax.tree.map(lambda _: VMEM, out),
        scratch_shapes=list(scratch),
        compiler_params=pltpu.CompilerParams(vmem_limit_bytes=vmem * 1024 * 1024),
        cost_estimate=pl.CostEstimate(flops=flops, bytes_accessed=2 * 1024 * 1024, transcendentals=0),
    )


def bf16(*shape):
    return jax.ShapeDtypeStruct(shape, BF)


def shards(forcing, legendre, assign, inverse, previous):
    x, core, rad = lax.axis_index("x"), lax.axis_index("core"), lax.axis_index(RAD)
    orders = assign.reshape(1, 256)
    place = jnp.stack([rad * 4 + x, (x * 2 + core) * 64 + rad, x, core]).astype(jnp.int32)

    sent = call(
        fourier_kernel,
        bf16(256, 2, 1280),
        [VMEM, HBM, HBM],
        [
            pltpu.VMEM((8, 96, LON), BF),
            pltpu.VMEM((8, 64, 512), BF),
            pltpu.VMEM((512, LON), BF),
            pltpu.VMEM((256, 2, 1280), BF),
            pltpu.SemaphoreType.DMA((2,)),
            pltpu.SemaphoreType.DMA((2,)),
        ],
        2 * 512 * 768 * 1024,
        60,
        HBM,
    )(orders, forcing, previous)
    sent, legendre = lax.optimization_barrier((sent, legendre))
    arrived = lax.all_to_all(sent, ("x",) + RAD, 0, 0, tiled=True)

    by_order = legendre.transpose(0, 2, 1)
    pieces = [lax.dynamic_index_in_dim(by_order, x, 0, keepdims=False)]
    for shift in range(1, 4):
        mine = lax.dynamic_index_in_dim(by_order, (x + shift) % 4, 0, keepdims=False)
        pieces.append(lax.ppermute(mine, "x", [(i, (i + shift) % 4) for i in range(4)]))
    own_weights, other_weights = call(
        legendre_kernel, (bf16(256, 640), bf16(256, 384)), [VMEM, SMEM, VMEM], (), 2 * 512 * 512 * 384
    )(orders, place, jnp.stack(pieces))
    solver, valid = call(
        inverse_kernel,
        (bf16(512, 512), jax.ShapeDtypeStruct((8, 512), F32)),
        [VMEM, SMEM, VMEM],
        (),
        2 * 512**3,
    )(orders, place, inverse)

    gathered, other = call(
        spectrum_kernel,
        (bf16(1024, 640), bf16(256, 1024)),
        [VMEM] * 2,
        [pltpu.VMEM((512, 1280), BF)],
        2 * 256 * 384 * 1024,
    )(arrived, other_weights)
    received = lax.all_gather(other, "core", axis=0)
    right = call(
        right_kernel, bf16(256, 2, 512), [SMEM, VMEM, VMEM, VMEM], (), 2 * 256 * 640 * 1024
    )(place, gathered, own_weights, received)
    right = lax.all_to_all(right, RAD + ("x",), 0, 0, tiled=True)
    solved = call(solve_kernel, bf16(512, 512), [VMEM] * 3, (), 2 * 512**3)(valid, solver, right)
    out = lax.all_to_all(solved.reshape(64, 8, 512), RAD, 0, 0, tiled=True)
    return out.transpose(1, 0, 2)


def solution(mesh):
    split = Mesh(mesh.devices.reshape(4, 2, 8, 8), LAT + RAD)
    placed = (
        P(RAD, LAT, None),
        P(RAD, None, LAT),
        P(),
        P(LAT + RAD, None, None),
        P(RAD, LAT, None),
    )
    return jax.shard_map(shards, mesh=split, in_specs=placed, out_specs=P(RAD, LAT, None), check_vma=False)
```

```python
import math

import jax
import jax.numpy as jnp
from jax import lax
from jax.experimental import pallas as pl
from jax.experimental.pallas import tpu as pltpu
from jax.sharding import Mesh, PartitionSpec as P

NR = 512
L = 512
LON = 1024
BF = jnp.bfloat16
F32 = jnp.float32
RAD = ("z", "y")
LAT = ("x", "core")


def nt_dot(a, b):
    return lax.dot_general(a, b, (((1,), (1,)), ((), ())), preferred_element_type=F32)


def iota(shape, dim):
    return lax.broadcasted_iota(jnp.int32, shape, dim)


def cos_sin(phase):
    quadrant = ((phase + 128) >> 8) & 3
    rest = ((phase + 128) & 255) - 128
    x = rest.astype(F32) * (2.0 * math.pi / LON)
    x2 = x * x
    sin_x = x * (1.0 + x2 * (-1.0 / 6 + x2 * (1.0 / 120 + x2 * (-1.0 / 5040 + x2 * (1.0 / 362880)))))
    cos_x = 1.0 + x2 * (-0.5 + x2 * (1.0 / 24 + x2 * (-1.0 / 720 + x2 * (1.0 / 40320))))
    swap = (quadrant & 1) == 1
    cos_part = jnp.where(swap, sin_x, cos_x)
    sin_part = jnp.where(swap, cos_x, sin_x)
    cos_sign = jnp.where((quadrant == 1) | (quadrant == 2), -1.0, 1.0)
    sin_sign = jnp.where(quadrant >= 2, -1.0, 1.0)
    return cos_part * cos_sign, sin_part * sin_sign


def fourier_kernel(
    assign_ref, forcing_hbm, previous_hbm, out_hbm, forcing_ref, previous_ref, table_ref, out_ref, in_sems, out_sems
):
    previous_copy = pltpu.make_async_copy(previous_hbm, previous_ref, in_sems.at[1])
    previous_copy.start()
    forcing_copy = pltpu.make_async_copy(forcing_hbm, forcing_ref, in_sems.at[0])
    forcing_copy.start()
    row = iota((512, 1), 0)
    slot = ((row >> 1) & 63) * 4 + (row >> 7)
    orders = jnp.sum(jnp.where(iota((512, 256), 1) == slot, assign_ref[...], 0), axis=1, keepdims=True)
    lane = iota((512, 128), 1)
    cos_now, sin_now = cos_sin((orders * lane + (row & 1) * (LON // 4)) & (LON - 1))
    cos_half, sin_half = cos_now[:, 64:65], sin_now[:, 64:65]
    sign = (1 - 2 * (row & 1)).astype(F32)
    cos_step = jnp.broadcast_to(sign * (1.0 - 2.0 * sin_half * sin_half), (512, 128))
    sin_step = jnp.broadcast_to(sign * (2.0 * sin_half * cos_half), (512, 128))
    cos_now, sin_now = cos_now * LON**-0.5, sin_now * LON**-0.5
    for q in range(LON // 128):
        table_ref[:, q * 128 : q * 128 + 128] = cos_now.astype(BF)
        cos_now, sin_now = cos_now * cos_step - sin_now * sin_step, sin_now * cos_step + cos_now * sin_step
    table = table_ref[...]
    reorder = (iota((512, 512), 1) == slot * 2 + (row & 1)).astype(BF)
    previous_copy.wait()
    previous = previous_ref[...].reshape(512, 512)
    forcing_copy.wait()
    out_copies = []
    for block in range(2):
        rows = slice(block * 256, block * 256 + 256)
        parts = []
        for h in range(3):
            part = forcing_ref[:, h * 32 : h * 32 + 32, :].reshape(256, LON)
            parts.append(nt_dot(table[rows], part).astype(BF))
        before = nt_dot(reorder[rows], previous).astype(BF)
        for half in range(2):
            dests = pl.ds(half * 256 + block * 128, 128)
            pieces = [part[:, half * 128 : half * 128 + 128] for part in parts]
            pieces.append(before[:, half * 256 : half * 256 + 256])
            out_ref[dests] = jnp.concatenate(pieces, axis=1).reshape(128, 2, 640)
            sem = out_sems.at[block * 2 + half]
            copy = pltpu.make_async_copy(out_ref.at[dests], out_hbm.at[dests], sem)
            copy.start()
            out_copies.append(copy)
    for copy in out_copies:
        copy.wait()


def legendre_kernel(assign_ref, place_ref, legendre_ref, out_ref, parted_ref):
    order = jnp.sum(jnp.where(iota((1, 256), 1) == place_ref[0], assign_ref[...], 0), axis=1, keepdims=True)
    row = iota((512, 1), 0)
    core, x, inner = row >> 8, row & 3, (row >> 2) & 63
    degree = (2 * x + core) * 64 + inner
    column = iota((512, 512), 1)
    kept = jnp.where((column == degree) & (degree >= order), 1.0, 0.0).astype(BF)
    x_here = place_ref[2]
    for h in range(3):
        rows = pl.ds(h * 32, 32)
        for core_from in range(2):
            pieces = [legendre_ref[core_from, (x_here - x_from) & 3, rows, :] for x_from in range(4)]
            at = h * 256 + core_from * 128
            out_ref[:, at : at + 128] = nt_dot(kept, jnp.concatenate(pieces, axis=0)).astype(BF)
    out_ref[:, 768:1280] = jnp.where(column == core * 256 + x * 64 + inner, 2.0, 0.0).astype(BF)
    parted_ref[...] = (column == (row & 1) * 256 + (row >> 1)).astype(BF)


def roll(a, shift):
    return pltpu.roll(a, shift, 1)


def spectrum_kernel(arrived_ref, weights_ref, parted_ref, out_ref, rows_ref, gathered_ref):
    rows_ref[...] = arrived_ref[...].reshape(1024, 640)
    lane = iota((128, 128), 1)
    low_half = lane < 64
    even_quarter = (lane & 32) == 0

    def tile(block, at):
        return rows_ref[block * 128 : block * 128 + 128, at : at + 128].astype(F32)

    def place(rho, at, value):
        gathered_ref[rho * 128 : rho * 128 + 128, at : at + 128] = value.astype(BF)

    for h in range(3):
        for core in range(2):
            a = [tile(core * 4 + x, h * 128) for x in range(4)]
            b0 = jnp.where(low_half, a[0], roll(a[2], 64))
            b2 = jnp.where(low_half, roll(a[0], 64), a[2])
            b1 = jnp.where(low_half, a[1], roll(a[3], 64))
            b3 = jnp.where(low_half, roll(a[1], 64), a[3])
            at = h * 256 + core * 128
            place(0, at, jnp.where(even_quarter, b0, roll(b1, 32)))
            place(1, at, jnp.where(even_quarter, roll(b0, 96), b1))
            place(2, at, jnp.where(even_quarter, b2, roll(b3, 32)))
            place(3, at, jnp.where(even_quarter, roll(b2, 96), b3))
    for pair in range(2):
        for two in range(4):
            at = 384 + pair * 128
            a0, a1 = tile(two * 2, at), tile(two * 2 + 1, at)
            to = 768 + two * 128
            place(pair * 2, to, jnp.where(low_half, a0, roll(a1, 64)))
            place(pair * 2 + 1, to, jnp.where(low_half, roll(a0, 64), a1))
    right = nt_dot(weights_ref[...], gathered_ref[...]).astype(BF)
    right = jnp.dot(right, parted_ref[...], preferred_element_type=F32).astype(BF)
    out_ref[...] = right.reshape(512, 2, 256)


def inverse_kernel(assign_ref, place_ref, inverse_ref, out_ref, valid_ref):
    inverse = inverse_ref[0].astype(BF)
    row, column = iota((256, 512), 0), iota((256, 512), 1)
    for half in range(2):
        radius = (row & 63) * 8 + half * 4 + (row >> 6)
        out_ref[half] = nt_dot(inverse, (column == radius).astype(BF)).astype(BF)
    valid = jnp.where(assign_ref[...] <= place_ref[1], 1.0, 0.0)
    doubled = (row == (column >> 1)).astype(BF)
    valid_ref[...] = jnp.dot(
        jnp.broadcast_to(valid, (8, 256)).astype(BF), doubled, preferred_element_type=F32
    )


def solve_kernel(valid_ref, inverse_ref, right_ref, out_ref):
    right = right_ref[...].reshape(1024, 256)
    solved = nt_dot(inverse_ref[0], right[:512]) + nt_dot(inverse_ref[1], right[512:])
    out_ref[...] = (solved * (valid_ref[0:1, :] * 0.5)).astype(BF)


VMEM = pl.BlockSpec(memory_space=pltpu.VMEM)
SMEM = pl.BlockSpec(memory_space=pltpu.SMEM)
HBM = pl.BlockSpec(memory_space=pltpu.HBM)


def call(kernel, out, ins, scratch=(), flops=0, vmem=24, outs=None):
    return pl.pallas_call(
        kernel,
        out_shape=out,
        in_specs=ins,
        out_specs=outs or jax.tree.map(lambda _: VMEM, out),
        scratch_shapes=list(scratch),
        compiler_params=pltpu.CompilerParams(vmem_limit_bytes=vmem * 1024 * 1024),
        cost_estimate=pl.CostEstimate(flops=flops, bytes_accessed=2 * 1024 * 1024, transcendentals=0),
    )


def bf16(*shape):
    return jax.ShapeDtypeStruct(shape, BF)


def shards(forcing, legendre, assign, inverse, previous):
    x, core, rad = lax.axis_index("x"), lax.axis_index("core"), lax.axis_index(RAD)
    orders = assign.reshape(1, 256)
    place = jnp.stack([rad * 4 + x, (x * 2 + core) * 64 + rad, x]).astype(jnp.int32)

    sent = call(
        fourier_kernel,
        bf16(512, 2, 640),
        [VMEM, HBM, HBM],
        [
            pltpu.VMEM((8, 96, LON), BF),
            pltpu.VMEM((8, 64, 512), BF),
            pltpu.VMEM((512, LON), BF),
            pltpu.VMEM((512, 2, 640), BF),
            pltpu.SemaphoreType.DMA((2,)),
            pltpu.SemaphoreType.DMA((4,)),
        ],
        2 * 512 * 768 * 1024,
        60,
        HBM,
    )(orders, forcing, previous)
    sent, legendre = lax.optimization_barrier((sent, legendre))
    arrived = lax.all_to_all(sent, ("core", "x") + RAD, 0, 0, tiled=True)

    by_order = legendre.transpose(0, 2, 1)
    pieces = [lax.dynamic_index_in_dim(by_order, x, 0, keepdims=False)]
    for shift in range(1, 4):
        mine = lax.dynamic_index_in_dim(by_order, (x + shift) % 4, 0, keepdims=False)
        pieces.append(lax.ppermute(mine, "x", [(i, (i + shift) % 4) for i in range(4)]))
    whole = lax.all_gather(jnp.stack(pieces), "core", axis=0)
    weights, parted = call(
        legendre_kernel, (bf16(512, 1280), bf16(512, 512)), [VMEM, SMEM, VMEM], (), 2 * 512 * 512 * 768
    )(orders, place, whole)
    solver, valid = call(
        inverse_kernel,
        (bf16(2, 512, 256), jax.ShapeDtypeStruct((8, 512), F32)),
        [VMEM, SMEM, VMEM],
        (),
        2 * 512**3,
    )(orders, place, inverse)

    weights, parted, solver, valid = lax.optimization_barrier((weights, parted, solver, valid))
    right = call(
        spectrum_kernel,
        bf16(512, 2, 256),
        [VMEM] * 3,
        [pltpu.VMEM((1024, 640), BF), pltpu.VMEM((512, 1280), BF)],
        2 * 512 * 512 * 1792,
    )(arrived, weights, parted)
    right = lax.all_to_all(right, ("core",) + RAD + ("x",), 0, 0, tiled=True)
    solved = call(solve_kernel, bf16(512, 512), [VMEM] * 3, (), 2 * 512**3)(valid, solver, right)
    out = lax.all_to_all(solved.reshape(64, 8, 512), RAD, 0, 0, tiled=True)
    return out.transpose(1, 0, 2)


def solution(mesh):
    split = Mesh(mesh.devices.reshape(4, 2, 8, 8), LAT + RAD)
    placed = (
        P(RAD, LAT, None),
        P(RAD, None, LAT),
        P(),
        P(LAT + RAD, None, None),
        P(RAD, LAT, None),
    )
    return jax.shard_map(shards, mesh=split, in_specs=placed, out_specs=P(RAD, LAT, None), check_vma=False)
```

```python
import math

import jax
import jax.numpy as jnp
from jax import lax
from jax.experimental import pallas as pl
from jax.experimental.pallas import tpu as pltpu
from jax.sharding import Mesh, PartitionSpec as P

NR = 512
L = 512
LON = 1024
BF = jnp.bfloat16
F32 = jnp.float32
RAD = ("z", "y")
LAT = ("x", "core")


def nt_dot(a, b):
    return lax.dot_general(a, b, (((1,), (1,)), ((), ())), preferred_element_type=F32)


def iota(shape, dim):
    return lax.broadcasted_iota(jnp.int32, shape, dim)


def cos_sin(phase):
    quadrant = ((phase + 128) >> 8) & 3
    rest = ((phase + 128) & 255) - 128
    x = rest.astype(F32) * (2.0 * math.pi / LON)
    x2 = x * x
    sin_x = x * (1.0 + x2 * (-1.0 / 6 + x2 * (1.0 / 120 + x2 * (-1.0 / 5040 + x2 * (1.0 / 362880)))))
    cos_x = 1.0 + x2 * (-0.5 + x2 * (1.0 / 24 + x2 * (-1.0 / 720 + x2 * (1.0 / 40320))))
    swap = (quadrant & 1) == 1
    cos_part = jnp.where(swap, sin_x, cos_x)
    sin_part = jnp.where(swap, cos_x, sin_x)
    cos_sign = jnp.where((quadrant == 1) | (quadrant == 2), -1.0, 1.0)
    sin_sign = jnp.where(quadrant >= 2, -1.0, 1.0)
    return cos_part * cos_sign, sin_part * sin_sign


def fourier_kernel(
    assign_ref, forcing_hbm, previous_hbm, out_hbm, forcing_ref, previous_ref, table_ref, out_ref, in_sems, out_sems
):
    previous_copy = pltpu.make_async_copy(previous_hbm, previous_ref, in_sems.at[1])
    previous_copy.start()
    forcing_copy = pltpu.make_async_copy(forcing_hbm, forcing_ref, in_sems.at[0])
    forcing_copy.start()
    row = iota((512, 1), 0)
    slot = ((row >> 1) & 63) * 4 + (row >> 7)
    orders = jnp.sum(jnp.where(iota((512, 256), 1) == slot, assign_ref[...], 0), axis=1, keepdims=True)
    lane = iota((512, 128), 1)
    cos_now, sin_now = cos_sin((orders * lane + (row & 1) * (LON // 4)) & (LON - 1))
    cos_half, sin_half = cos_now[:, 64:65], sin_now[:, 64:65]
    sign = (1 - 2 * (row & 1)).astype(F32)
    cos_step = jnp.broadcast_to(sign * (1.0 - 2.0 * sin_half * sin_half), (512, 128))
    sin_step = jnp.broadcast_to(sign * (2.0 * sin_half * cos_half), (512, 128))
    cos_now, sin_now = cos_now * LON**-0.5, sin_now * LON**-0.5
    for q in range(LON // 128):
        table_ref[:, q * 128 : q * 128 + 128] = cos_now.astype(BF)
        cos_now, sin_now = cos_now * cos_step - sin_now * sin_step, sin_now * cos_step + cos_now * sin_step
    table = table_ref[...]
    reorder = (iota((512, 512), 1) == slot * 2 + (row & 1)).astype(BF)
    previous_copy.wait()
    previous = previous_ref[...].reshape(512, 512)
    forcing_copy.wait()
    out_copies = []
    for block in range(2):
        rows = slice(block * 256, block * 256 + 256)
        parts = []
        for h in range(3):
            part = forcing_ref[:, h * 32 : h * 32 + 32, :].reshape(256, LON)
            parts.append(nt_dot(table[rows], part).astype(BF))
        before = nt_dot(reorder[rows], previous).astype(BF)
        for half in range(2):
            dests = pl.ds(half * 256 + block * 128, 128)
            pieces = [part[:, half * 128 : half * 128 + 128] for part in parts]
            pieces.append(before[:, half * 256 : half * 256 + 256])
            out_ref[dests] = jnp.concatenate(pieces, axis=1).reshape(128, 2, 640)
            sem = out_sems.at[block * 2 + half]
            copy = pltpu.make_async_copy(out_ref.at[dests], out_hbm.at[dests], sem)
            copy.start()
            out_copies.append(copy)
    for copy in out_copies:
        copy.wait()


def legendre_kernel(assign_ref, place_ref, legendre_ref, out_ref):
    order = jnp.sum(jnp.where(iota((1, 256), 1) == place_ref[0], assign_ref[...], 0), axis=1, keepdims=True)
    row = iota((512, 1), 0)
    core, x, inner = row >> 8, row & 3, (row >> 2) & 63
    degree = (2 * x + core) * 64 + inner
    column = iota((512, 512), 1)
    kept = jnp.where((column == degree) & (degree >= order), 1.0, 0.0).astype(BF)
    x_here = place_ref[2]
    for h in range(3):
        rows = pl.ds(h * 32, 32)
        for core_from in range(2):
            pieces = [legendre_ref[core_from, (x_here - x_from) & 3, rows, :] for x_from in range(4)]
            at = h * 256 + core_from * 128
            out_ref[:, at : at + 128] = nt_dot(kept, jnp.concatenate(pieces, axis=0)).astype(BF)
    out_ref[:, 768:1280] = jnp.where(column == core * 256 + x * 64 + inner, 2.0, 0.0).astype(BF)


def roll(a, shift):
    return pltpu.roll(a, shift, 1)


def spectrum_kernel(arrived_ref, weights_ref, out_ref, rows_ref, gathered_ref):
    rows_ref[...] = arrived_ref[...].reshape(1024, 640)
    lane = iota((128, 128), 1)
    low_half = lane < 64
    even_quarter = (lane & 32) == 0

    def tile(block, at):
        return rows_ref[block * 128 : block * 128 + 128, at : at + 128].astype(F32)

    def place(rho, at, value):
        gathered_ref[rho * 128 : rho * 128 + 128, at : at + 128] = value.astype(BF)

    for h in range(3):
        for core in range(2):
            a = [tile(core * 4 + x, h * 128) for x in range(4)]
            b0 = jnp.where(low_half, a[0], roll(a[2], 64))
            b2 = jnp.where(low_half, roll(a[0], 64), a[2])
            b1 = jnp.where(low_half, a[1], roll(a[3], 64))
            b3 = jnp.where(low_half, roll(a[1], 64), a[3])
            at = h * 256 + core * 128
            place(0, at, jnp.where(even_quarter, b0, roll(b1, 32)))
            place(1, at, jnp.where(even_quarter, roll(b0, 96), b1))
            place(2, at, jnp.where(even_quarter, b2, roll(b3, 32)))
            place(3, at, jnp.where(even_quarter, roll(b2, 96), b3))
    for pair in range(2):
        for two in range(4):
            at = 384 + pair * 128
            a0, a1 = tile(two * 2, at), tile(two * 2 + 1, at)
            to = 768 + two * 128
            place(pair * 2, to, jnp.where(low_half, a0, roll(a1, 64)))
            place(pair * 2 + 1, to, jnp.where(low_half, roll(a0, 64), a1))
    right = nt_dot(weights_ref[...], gathered_ref[...]).astype(BF)
    row, column = iota((256, 1), 0), iota((256, 256), 1)
    parted = (column == (row & 1) * 128 + (row >> 1)).astype(BF)
    parts = []
    for i in range(2):
        part = right[:, i * 256 : i * 256 + 256]
        parts.append(jnp.dot(part, parted, preferred_element_type=F32).astype(BF))
    parts = [part[:, :128] for part in parts] + [part[:, 128:] for part in parts]
    out_ref[...] = jnp.concatenate(parts, axis=1).reshape(512, 2, 256)


def inverse_kernel(assign_ref, place_ref, inverse_ref, out_ref, valid_ref):
    inverse = inverse_ref[0].astype(BF)
    row, column = iota((256, 512), 0), iota((256, 512), 1)
    for half in range(2):
        radius = (row & 63) * 8 + half * 4 + (row >> 6)
        out_ref[half] = nt_dot(inverse, (column == radius).astype(BF)).astype(BF)
    valid = jnp.where(assign_ref[...] <= place_ref[1], 1.0, 0.0)
    doubled = (row == (column >> 1)).astype(BF)
    valid_ref[...] = jnp.dot(
        jnp.broadcast_to(valid, (8, 256)).astype(BF), doubled, preferred_element_type=F32
    )


def solve_kernel(valid_ref, inverse_ref, right_ref, out_ref):
    right = right_ref[...].reshape(1024, 256)
    solved = nt_dot(inverse_ref[0], right[:512]) + nt_dot(inverse_ref[1], right[512:])
    out_ref[...] = (solved * (valid_ref[0:1, :] * 0.5)).astype(BF)


VMEM = pl.BlockSpec(memory_space=pltpu.VMEM)
SMEM = pl.BlockSpec(memory_space=pltpu.SMEM)
HBM = pl.BlockSpec(memory_space=pltpu.HBM)


def call(kernel, out, ins, scratch=(), flops=0, vmem=16, outs=None):
    return pl.pallas_call(
        kernel,
        out_shape=out,
        in_specs=ins,
        out_specs=outs or jax.tree.map(lambda _: VMEM, out),
        scratch_shapes=list(scratch),
        compiler_params=pltpu.CompilerParams(vmem_limit_bytes=vmem * 1024 * 1024),
        cost_estimate=pl.CostEstimate(flops=flops, bytes_accessed=2 * 1024 * 1024, transcendentals=0),
    )


def bf16(*shape):
    return jax.ShapeDtypeStruct(shape, BF)


def shards(forcing, legendre, assign, inverse, previous):
    x, core, rad = lax.axis_index("x"), lax.axis_index("core"), lax.axis_index(RAD)
    orders = assign.reshape(1, 256)
    place = jnp.stack([rad * 4 + x, (x * 2 + core) * 64 + rad, x]).astype(jnp.int32)

    sent = call(
        fourier_kernel,
        bf16(512, 2, 640),
        [VMEM, HBM, HBM],
        [
            pltpu.VMEM((8, 96, LON), BF),
            pltpu.VMEM((8, 64, 512), BF),
            pltpu.VMEM((512, LON), BF),
            pltpu.VMEM((512, 2, 640), BF),
            pltpu.SemaphoreType.DMA((2,)),
            pltpu.SemaphoreType.DMA((4,)),
        ],
        2 * 512 * 768 * 1024,
        60,
        HBM,
    )(orders, forcing, previous)
    sent, legendre = lax.optimization_barrier((sent, legendre))
    arrived = lax.all_to_all(sent, ("core", "x") + RAD, 0, 0, tiled=True)

    by_order = legendre.transpose(0, 2, 1)
    pieces = [lax.dynamic_index_in_dim(by_order, x, 0, keepdims=False)]
    for shift in range(1, 4):
        mine = lax.dynamic_index_in_dim(by_order, (x + shift) % 4, 0, keepdims=False)
        pieces.append(lax.ppermute(mine, "x", [(i, (i + shift) % 4) for i in range(4)]))
    whole = lax.all_gather(jnp.stack(pieces), "core", axis=0)
    weights = call(legendre_kernel, bf16(512, 1280), [VMEM, SMEM, VMEM], (), 2 * 512 * 512 * 768)(
        orders, place, whole
    )
    solver, valid = call(
        inverse_kernel,
        (bf16(2, 512, 256), jax.ShapeDtypeStruct((8, 512), F32)),
        [VMEM, SMEM, VMEM],
        (),
        2 * 512**3,
    )(orders, place, inverse)

    weights, solver, valid = lax.optimization_barrier((weights, solver, valid))
    right = call(
        spectrum_kernel,
        bf16(512, 2, 256),
        [VMEM] * 2,
        [pltpu.VMEM((1024, 640), BF), pltpu.VMEM((512, 1280), BF)],
        2 * 512 * 512 * 1536,
    )(arrived, weights)
    right = lax.all_to_all(right, ("core",) + RAD + ("x",), 0, 0, tiled=True)
    solved = call(solve_kernel, bf16(512, 512), [VMEM] * 3, (), 2 * 512**3)(valid, solver, right)
    out = lax.all_to_all(solved.reshape(64, 8, 512), RAD, 0, 0, tiled=True)
    return out.transpose(1, 0, 2)


def solution(mesh):
    split = Mesh(mesh.devices.reshape(4, 2, 8, 8), LAT + RAD)
    placed = (
        P(RAD, LAT, None),
        P(RAD, None, LAT),
        P(),
        P(LAT + RAD, None, None),
        P(RAD, LAT, None),
    )
    return jax.shard_map(shards, mesh=split, in_specs=placed, out_specs=P(RAD, LAT, None), check_vma=False)
```

```python
import math

import jax
import jax.numpy as jnp
from jax import lax
from jax.experimental import pallas as pl
from jax.experimental.pallas import tpu as pltpu
from jax.sharding import Mesh, PartitionSpec as P

NR = 512
L = 512
LON = 1024
BF = jnp.bfloat16
F32 = jnp.float32
RAD = ("z", "y")
LAT = ("x", "core")


def nt_dot(a, b):
    return lax.dot_general(a, b, (((1,), (1,)), ((), ())), preferred_element_type=F32)


def iota(shape, dim):
    return lax.broadcasted_iota(jnp.int32, shape, dim)


def cos_sin(phase):
    quadrant = ((phase + 128) >> 8) & 3
    rest = ((phase + 128) & 255) - 128
    x = rest.astype(F32) * (2.0 * math.pi / LON)
    x2 = x * x
    sin_x = x * (1.0 + x2 * (-1.0 / 6 + x2 * (1.0 / 120 + x2 * (-1.0 / 5040 + x2 * (1.0 / 362880)))))
    cos_x = 1.0 + x2 * (-0.5 + x2 * (1.0 / 24 + x2 * (-1.0 / 720 + x2 * (1.0 / 40320))))
    swap = (quadrant & 1) == 1
    cos_part = jnp.where(swap, sin_x, cos_x)
    sin_part = jnp.where(swap, cos_x, sin_x)
    cos_sign = jnp.where((quadrant == 1) | (quadrant == 2), -1.0, 1.0)
    sin_sign = jnp.where(quadrant >= 2, -1.0, 1.0)
    return cos_part * cos_sign, sin_part * sin_sign


def fourier_kernel(
    assign_ref, forcing_hbm, previous_hbm, out_hbm, forcing_ref, previous_ref, table_ref, out_ref, in_sems, out_sems
):
    previous_copy = pltpu.make_async_copy(previous_hbm, previous_ref, in_sems.at[1])
    previous_copy.start()
    forcing_copy = pltpu.make_async_copy(forcing_hbm, forcing_ref, in_sems.at[0])
    forcing_copy.start()
    row = iota((512, 1), 0)
    slot = ((row >> 1) & 63) * 4 + (row >> 7)
    orders = jnp.sum(jnp.where(iota((512, 256), 1) == slot, assign_ref[...], 0), axis=1, keepdims=True)
    lane = iota((512, 128), 1)
    cos_now, sin_now = cos_sin((orders * lane + (row & 1) * (LON // 4)) & (LON - 1))
    cos_half, sin_half = cos_now[:, 64:65], sin_now[:, 64:65]
    sign = (1 - 2 * (row & 1)).astype(F32)
    cos_step = jnp.broadcast_to(sign * (1.0 - 2.0 * sin_half * sin_half), (512, 128))
    sin_step = jnp.broadcast_to(sign * (2.0 * sin_half * cos_half), (512, 128))
    cos_now, sin_now = cos_now * LON**-0.5, sin_now * LON**-0.5
    for q in range(LON // 128):
        table_ref[:, q * 128 : q * 128 + 128] = cos_now.astype(BF)
        cos_now, sin_now = cos_now * cos_step - sin_now * sin_step, sin_now * cos_step + cos_now * sin_step
    table = table_ref[...]
    reorder = (iota((512, 512), 1) == slot * 2 + (row & 1)).astype(BF)
    previous_copy.wait()
    previous = previous_ref[...].reshape(512, 512)
    forcing_copy.wait()
    out_copies = []
    for block in range(2):
        rows = slice(block * 256, block * 256 + 256)
        parts = []
        for h in range(3):
            part = forcing_ref[:, h * 32 : h * 32 + 32, :].reshape(256, LON)
            parts.append(nt_dot(table[rows], part).astype(BF))
        parts.append(nt_dot(reorder[rows], previous).astype(BF))
        dests = pl.ds(block * 128, 128)
        out_ref[dests] = jnp.concatenate(parts, axis=1).reshape(128, 2, 1280)
        copy = pltpu.make_async_copy(out_ref.at[dests], out_hbm.at[dests], out_sems.at[block])
        copy.start()
        out_copies.append(copy)
    for copy in out_copies:
        copy.wait()


def legendre_kernel(assign_ref, place_ref, legendre_ref, own_ref, other_ref):
    order = jnp.sum(jnp.where(iota((1, 256), 1) == place_ref[0], assign_ref[...], 0), axis=1, keepdims=True)
    x_here, core = place_ref[2], place_ref[3]
    row, column = iota((256, 1), 0), iota((256, 512), 1)
    x, rad = row & 3, row >> 2
    kept = []
    for of_core in (core, 1 - core):
        degree = (2 * x + of_core) * 64 + rad
        kept.append(jnp.where((column == degree) & (degree >= order), 1.0, 0.0).astype(BF))
    for h in range(3):
        pieces = [legendre_ref[(x_here - x_from) & 3, h * 32 : h * 32 + 32, :] for x_from in range(4)]
        pieces = jnp.concatenate(pieces, axis=0)
        own_ref[:, h * 128 : h * 128 + 128] = nt_dot(kept[0], pieces).astype(BF)
        other_ref[:, h * 128 : h * 128 + 128] = nt_dot(kept[1], pieces).astype(BF)
    own_ref[:, 384:640] = jnp.where(iota((256, 256), 1) == x * 64 + rad, 2.0, 0.0).astype(BF)


def roll(a, shift):
    return pltpu.roll(a, shift, 1)


def spectrum_kernel(arrived_ref, weights_ref, gathered_ref, first_ref, second_ref, rows_ref):
    rows_ref[...] = arrived_ref[...].reshape(512, 1280)
    lane = iota((128, 128), 1)
    low_half = lane < 64
    even_quarter = (lane & 32) == 0

    def tile(block, at):
        return rows_ref[block * 128 : block * 128 + 128, at : at + 128].astype(F32)

    def place(rho, at, value):
        gathered_ref[rho * 128 : rho * 128 + 128, at : at + 128] = value.astype(BF)

    for h in range(3):
        for high in range(2):
            a = [tile(x, h * 256 + high * 128) for x in range(4)]
            b0 = jnp.where(low_half, a[0], roll(a[2], 64))
            b2 = jnp.where(low_half, roll(a[0], 64), a[2])
            b1 = jnp.where(low_half, a[1], roll(a[3], 64))
            b3 = jnp.where(low_half, roll(a[1], 64), a[3])
            at, rho = h * 128, high * 4
            place(rho, at, jnp.where(even_quarter, b0, roll(b1, 32)))
            place(rho + 1, at, jnp.where(even_quarter, roll(b0, 96), b1))
            place(rho + 2, at, jnp.where(even_quarter, b2, roll(b3, 32)))
            place(rho + 3, at, jnp.where(even_quarter, roll(b2, 96), b3))
    other = nt_dot(weights_ref[...], gathered_ref[:, :384]).astype(BF)
    first_ref[...] = other[:128]
    second_ref[...] = other[128:]
    for pair in range(4):
        for two in range(2):
            at = 768 + pair * 128
            a0, a1 = tile(two * 2, at), tile(two * 2 + 1, at)
            to = 384 + two * 128
            place(pair * 2, to, jnp.where(low_half, a0, roll(a1, 64)))
            place(pair * 2 + 1, to, jnp.where(low_half, roll(a0, 64), a1))


def right_kernel(place_ref, gathered_ref, weights_ref, first_ref, second_ref, out_ref):
    own = nt_dot(weights_ref[...], gathered_ref[...])
    from_core = 1 - place_ref[3]
    received = jnp.concatenate([first_ref[from_core], second_ref[from_core]], axis=0)
    right = (own + received.astype(F32)).astype(BF)
    row, column = iota((256, 256), 0), iota((256, 256), 1)
    parted = (column == (row & 1) * 128 + (row >> 1)).astype(BF)
    parts = []
    for i in range(4):
        part = right[:, i * 256 : i * 256 + 256]
        parts.append(jnp.dot(part, parted, preferred_element_type=F32).astype(BF))
    parts = [part[:, :128] for part in parts] + [part[:, 128:] for part in parts]
    out_ref[...] = jnp.concatenate(parts, axis=1).reshape(256, 2, 512)


def inverse_kernel(assign_ref, place_ref, inverse_ref, out_ref, valid_ref):
    row, column = iota((512, 1), 0), iota((512, 512), 1)
    regroup = (column == (row & 63) * 8 + (row >> 6)).astype(BF)
    out_ref[...] = nt_dot(inverse_ref[0].astype(BF), regroup).astype(BF)
    valid = jnp.where(assign_ref[...] <= place_ref[1], 1.0, 0.0)
    row, column = iota((256, 512), 0), iota((256, 512), 1)
    doubled = (row == (column >> 1)).astype(BF)
    valid_ref[...] = jnp.dot(
        jnp.broadcast_to(valid, (8, 256)).astype(BF), doubled, preferred_element_type=F32
    )


def solve_kernel(valid_ref, inverse_ref, right_ref, out_ref):
    solved = nt_dot(inverse_ref[...], right_ref[...].reshape(512, 512))
    out_ref[...] = (solved * (valid_ref[0:1, :] * 0.5)).astype(BF)


VMEM = pl.BlockSpec(memory_space=pltpu.VMEM)
SMEM = pl.BlockSpec(memory_space=pltpu.SMEM)
HBM = pl.BlockSpec(memory_space=pltpu.HBM)


def call(kernel, out, ins, scratch=(), flops=0, vmem=16, outs=None):
    return pl.pallas_call(
        kernel,
        out_shape=out,
        in_specs=ins,
        out_specs=outs or jax.tree.map(lambda _: VMEM, out),
        scratch_shapes=list(scratch),
        compiler_params=pltpu.CompilerParams(vmem_limit_bytes=vmem * 1024 * 1024),
        cost_estimate=pl.CostEstimate(flops=flops, bytes_accessed=2 * 1024 * 1024, transcendentals=0),
    )


def bf16(*shape):
    return jax.ShapeDtypeStruct(shape, BF)


def shards(forcing, legendre, assign, inverse, previous):
    x, core, rad = lax.axis_index("x"), lax.axis_index("core"), lax.axis_index(RAD)
    orders = assign.reshape(1, 256)
    place = jnp.stack([rad * 4 + x, (x * 2 + core) * 64 + rad, x, core]).astype(jnp.int32)

    sent = call(
        fourier_kernel,
        bf16(256, 2, 1280),
        [VMEM, HBM, HBM],
        [
            pltpu.VMEM((8, 96, LON), BF),
            pltpu.VMEM((8, 64, 512), BF),
            pltpu.VMEM((512, LON), BF),
            pltpu.VMEM((256, 2, 1280), BF),
            pltpu.SemaphoreType.DMA((2,)),
            pltpu.SemaphoreType.DMA((2,)),
        ],
        2 * 512 * 768 * 1024,
        60,
        HBM,
    )(orders, forcing, previous)
    sent, legendre = lax.optimization_barrier((sent, legendre))
    arrived = lax.all_to_all(sent, ("x",) + RAD, 0, 0, tiled=True)

    by_order = legendre.transpose(0, 2, 1)
    pieces = [lax.dynamic_index_in_dim(by_order, x, 0, keepdims=False)]
    for shift in range(1, 4):
        mine = lax.dynamic_index_in_dim(by_order, (x + shift) % 4, 0, keepdims=False)
        pieces.append(lax.ppermute(mine, "x", [(i, (i + shift) % 4) for i in range(4)]))
    own_weights, other_weights = call(
        legendre_kernel, (bf16(256, 640), bf16(256, 384)), [VMEM, SMEM, VMEM], (), 2 * 512 * 512 * 384
    )(orders, place, jnp.stack(pieces))
    solver, valid = call(
        inverse_kernel,
        (bf16(512, 512), jax.ShapeDtypeStruct((8, 512), F32)),
        [VMEM, SMEM, VMEM],
        (),
        2 * 512**3,
    )(orders, place, inverse)

    own_weights, other_weights, solver, valid = lax.optimization_barrier(
        (own_weights, other_weights, solver, valid)
    )
    gathered, first, second = call(
        spectrum_kernel,
        (bf16(1024, 640), bf16(128, 1024), bf16(128, 1024)),
        [VMEM] * 2,
        [pltpu.VMEM((512, 1280), BF)],
        2 * 256 * 384 * 1024,
    )(arrived, other_weights)
    first = lax.all_gather(first, "core", axis=0)
    first, second = lax.optimization_barrier((first, second))
    second = lax.all_gather(second, "core", axis=0)
    right = call(
        right_kernel, bf16(256, 2, 512), [SMEM, VMEM, VMEM, VMEM, VMEM], (), 2 * 256 * 640 * 1024
    )(place, gathered, own_weights, first, second)
    right = lax.all_to_all(right, RAD + ("x",), 0, 0, tiled=True)
    solved = call(solve_kernel, bf16(512, 512), [VMEM] * 3, (), 2 * 512**3)(valid, solver, right)
    out = lax.all_to_all(solved.reshape(64, 8, 512), RAD, 0, 0, tiled=True)
    return out.transpose(1, 0, 2)


def solution(mesh):
    split = Mesh(mesh.devices.reshape(4, 2, 8, 8), LAT + RAD)
    placed = (
        P(RAD, LAT, None),
        P(RAD, None, LAT),
        P(),
        P(LAT + RAD, None, None),
        P(RAD, LAT, None),
    )
    return jax.shard_map(shards, mesh=split, in_specs=placed, out_specs=P(RAD, LAT, None), check_vma=False)
```

```python
import math

import jax
import jax.numpy as jnp
from jax import lax
from jax.experimental import pallas as pl
from jax.experimental.pallas import tpu as pltpu
from jax.sharding import Mesh, PartitionSpec as P

NR = 512
L = 512
LON = 1024
BF = jnp.bfloat16
F32 = jnp.float32
RAD = ("z", "y")
LAT = ("x", "core")


def nt_dot(a, b):
    return lax.dot_general(a, b, (((1,), (1,)), ((), ())), preferred_element_type=F32)


def iota(shape, dim):
    return lax.broadcasted_iota(jnp.int32, shape, dim)


def cos_sin(phase):
    quadrant = ((phase + 128) >> 8) & 3
    rest = ((phase + 128) & 255) - 128
    x = rest.astype(F32) * (2.0 * math.pi / LON)
    x2 = x * x
    sin_x = x * (1.0 + x2 * (-1.0 / 6 + x2 * (1.0 / 120 + x2 * (-1.0 / 5040 + x2 * (1.0 / 362880)))))
    cos_x = 1.0 + x2 * (-0.5 + x2 * (1.0 / 24 + x2 * (-1.0 / 720 + x2 * (1.0 / 40320))))
    swap = (quadrant & 1) == 1
    cos_part = jnp.where(swap, sin_x, cos_x)
    sin_part = jnp.where(swap, cos_x, sin_x)
    cos_sign = jnp.where((quadrant == 1) | (quadrant == 2), -1.0, 1.0)
    sin_sign = jnp.where(quadrant >= 2, -1.0, 1.0)
    return cos_part * cos_sign, sin_part * sin_sign


def fourier_kernel(
    assign_ref, forcing_hbm, previous_hbm, out_hbm, forcing_ref, previous_ref, table_ref, out_ref, in_sems, out_sems
):
    previous_copy = pltpu.make_async_copy(previous_hbm, previous_ref, in_sems.at[1])
    previous_copy.start()
    forcing_copy = pltpu.make_async_copy(forcing_hbm, forcing_ref, in_sems.at[0])
    forcing_copy.start()
    row = iota((512, 1), 0)
    slot = row >> 1
    orders = jnp.sum(jnp.where(iota((512, 256), 1) == slot, assign_ref[...], 0), axis=1, keepdims=True)
    lane = iota((512, 128), 1)
    cos_now, sin_now = cos_sin((orders * lane + (row & 1) * (LON // 4)) & (LON - 1))
    cos_half, sin_half = cos_now[:, 64:65], sin_now[:, 64:65]
    sign = (1 - 2 * (row & 1)).astype(F32)
    cos_step = jnp.broadcast_to(sign * (1.0 - 2.0 * sin_half * sin_half), (512, 128))
    sin_step = jnp.broadcast_to(sign * (2.0 * sin_half * cos_half), (512, 128))
    cos_now, sin_now = cos_now * LON**-0.5, sin_now * LON**-0.5
    for q in range(LON // 128):
        table_ref[:, q * 128 : q * 128 + 128] = cos_now.astype(BF)
        cos_now, sin_now = cos_now * cos_step - sin_now * sin_step, sin_now * cos_step + cos_now * sin_step
    table = table_ref[...]
    previous_copy.wait()
    previous = previous_ref[...].reshape(512, 512).T
    forcing_copy.wait()
    out_copies = []
    for block in range(2):
        rows = slice(block * 256, block * 256 + 256)
        parts = []
        for h in range(3):
            part = forcing_ref[:, h * 32 : h * 32 + 32, :].reshape(256, LON)
            parts.append(nt_dot(table[rows], part).astype(BF))
        before = previous[rows]
        for half in range(2):
            dests = pl.ds(half * 256 + block * 128, 128)
            pieces = [part[:, half * 128 : half * 128 + 128] for part in parts]
            pieces.append(before[:, half * 256 : half * 256 + 256])
            out_ref[dests] = jnp.concatenate(pieces, axis=1).reshape(128, 2, 640)
            sem = out_sems.at[block * 2 + half]
            copy = pltpu.make_async_copy(out_ref.at[dests], out_hbm.at[dests], sem)
            copy.start()
            out_copies.append(copy)
    for copy in out_copies:
        copy.wait()


def legendre_kernel(assign_ref, place_ref, legendre_ref, out_ref):
    order = jnp.sum(jnp.where(iota((1, 256), 1) == place_ref[0], assign_ref[...], 0), axis=1, keepdims=True)
    row = iota((512, 1), 0)
    core, x, inner = row >> 8, row & 3, (row >> 2) & 63
    degree = (2 * x + core) * 64 + inner
    column = iota((512, 512), 1)
    kept = jnp.where((column == degree) & (degree >= order), 1.0, 0.0).astype(BF)
    x_here = place_ref[2]
    for h in range(3):
        rows = pl.ds(h * 32, 32)
        for core_from in range(2):
            pieces = [legendre_ref[core_from, (x_here - x_from) & 3, rows, :] for x_from in range(4)]
            at = h * 256 + core_from * 128
            out_ref[:, at : at + 128] = nt_dot(kept, jnp.concatenate(pieces, axis=0)).astype(BF)
    out_ref[:, 768:1280] = jnp.where(column == core * 256 + x * 64 + inner, 2.0, 0.0).astype(BF)


def roll(a, shift):
    return pltpu.roll(a, shift, 1)


def spectrum_kernel(arrived_ref, weights_ref, out_ref, rows_ref, gathered_ref):
    for block in range(8):
        rows = slice(block * 128, block * 128 + 128)
        rows_ref[rows] = arrived_ref[block // 4, :, block % 4].reshape(128, 640)
    lane = iota((128, 128), 1)
    low_half = lane < 64
    even_quarter = (lane & 32) == 0

    def tile(block, at):
        return rows_ref[block * 128 : block * 128 + 128, at : at + 128].astype(F32)

    def place(rho, at, value):
        gathered_ref[rho * 128 : rho * 128 + 128, at : at + 128] = value.astype(BF)

    for h in range(3):
        for core in range(2):
            a = [tile(core * 4 + x, h * 128) for x in range(4)]
            b0 = jnp.where(low_half, a[0], roll(a[2], 64))
            b2 = jnp.where(low_half, roll(a[0], 64), a[2])
            b1 = jnp.where(low_half, a[1], roll(a[3], 64))
            b3 = jnp.where(low_half, roll(a[1], 64), a[3])
            at = h * 256 + core * 128
            place(0, at, jnp.where(even_quarter, b0, roll(b1, 32)))
            place(1, at, jnp.where(even_quarter, roll(b0, 96), b1))
            place(2, at, jnp.where(even_quarter, b2, roll(b3, 32)))
            place(3, at, jnp.where(even_quarter, roll(b2, 96), b3))
    for pair in range(2):
        for two in range(4):
            at = 384 + pair * 128
            a0, a1 = tile(two * 2, at), tile(two * 2 + 1, at)
            to = 768 + two * 128
            place(pair * 2, to, jnp.where(low_half, a0, roll(a1, 64)))
            place(pair * 2 + 1, to, jnp.where(low_half, roll(a0, 64), a1))
    right = nt_dot(weights_ref[...], gathered_ref[...]).astype(BF)
    row, column = iota((256, 1), 0), iota((256, 256), 1)
    parted = (column == (row & 1) * 128 + (row >> 1)).astype(BF)
    parts = []
    for i in range(2):
        part = right[:, i * 256 : i * 256 + 256]
        parts.append(jnp.dot(part, parted, preferred_element_type=F32).astype(BF))
    parts = [part[:, :128] for part in parts] + [part[:, 128:] for part in parts]
    out_ref[...] = jnp.concatenate(parts, axis=1).reshape(512, 2, 256)


def inverse_kernel(assign_ref, place_ref, inverse_ref, out_ref, valid_ref):
    inverse = inverse_ref[0].astype(BF)
    row, column = iota((256, 512), 0), iota((256, 512), 1)
    for half in range(2):
        radius = (row & 63) * 8 + half * 4 + (row >> 6)
        out_ref[half] = nt_dot(inverse, (column == radius).astype(BF)).astype(BF)
    valid = jnp.where(assign_ref[...] <= place_ref[1], 1.0, 0.0)
    doubled = (row == (column >> 1)).astype(BF)
    valid_ref[...] = jnp.dot(
        jnp.broadcast_to(valid, (8, 256)).astype(BF), doubled, preferred_element_type=F32
    )


def solve_kernel(valid_ref, inverse_ref, right_ref, out_ref):
    right = right_ref[...].reshape(1024, 256)
    solved = nt_dot(inverse_ref[0], right[:512]) + nt_dot(inverse_ref[1], right[512:])
    out_ref[...] = (solved * (valid_ref[0:1, :] * 0.5)).astype(BF)


VMEM = pl.BlockSpec(memory_space=pltpu.VMEM)
SMEM = pl.BlockSpec(memory_space=pltpu.SMEM)
HBM = pl.BlockSpec(memory_space=pltpu.HBM)


def call(kernel, out, ins, scratch=(), flops=0, vmem=16, outs=None):
    return pl.pallas_call(
        kernel,
        out_shape=out,
        in_specs=ins,
        out_specs=outs or jax.tree.map(lambda _: VMEM, out),
        scratch_shapes=list(scratch),
        compiler_params=pltpu.CompilerParams(vmem_limit_bytes=vmem * 1024 * 1024),
        cost_estimate=pl.CostEstimate(flops=flops, bytes_accessed=2 * 1024 * 1024, transcendentals=0),
    )


def bf16(*shape):
    return jax.ShapeDtypeStruct(shape, BF)


def shards(forcing, legendre, assign, inverse, previous):
    x, core, rad = lax.axis_index("x"), lax.axis_index("core"), lax.axis_index(RAD)
    orders = assign.reshape(1, 256)
    place = jnp.stack([rad * 4 + x, (x * 2 + core) * 64 + rad, x]).astype(jnp.int32)

    sent = call(
        fourier_kernel,
        bf16(512, 2, 640),
        [VMEM, HBM, HBM],
        [
            pltpu.VMEM((8, 96, LON), BF),
            pltpu.VMEM((8, 64, 512), BF),
            pltpu.VMEM((512, LON), BF),
            pltpu.VMEM((512, 2, 640), BF),
            pltpu.SemaphoreType.DMA((2,)),
            pltpu.SemaphoreType.DMA((4,)),
        ],
        2 * 512 * 768 * 1024,
        60,
        HBM,
    )(orders, forcing, previous)
    sent, legendre = lax.optimization_barrier((sent, legendre))
    arrived = lax.all_to_all(sent, ("core",) + RAD + ("x",), 0, 0, tiled=True)

    by_order = legendre.transpose(0, 2, 1)
    pieces = [lax.dynamic_index_in_dim(by_order, x, 0, keepdims=False)]
    for shift in range(1, 4):
        mine = lax.dynamic_index_in_dim(by_order, (x + shift) % 4, 0, keepdims=False)
        pieces.append(lax.ppermute(mine, "x", [(i, (i + shift) % 4) for i in range(4)]))
    whole = lax.all_gather(jnp.stack(pieces), "core", axis=0)
    weights = call(legendre_kernel, bf16(512, 1280), [VMEM, SMEM, VMEM], (), 2 * 512 * 512 * 768)(
        orders, place, whole
    )
    solver, valid = call(
        inverse_kernel,
        (bf16(2, 512, 256), jax.ShapeDtypeStruct((8, 512), F32)),
        [VMEM, SMEM, VMEM],
        (),
        2 * 512**3,
    )(orders, place, inverse)

    weights, solver, valid = lax.optimization_barrier((weights, solver, valid))
    right = call(
        spectrum_kernel,
        bf16(512, 2, 256),
        [VMEM] * 2,
        [pltpu.VMEM((1024, 640), BF), pltpu.VMEM((512, 1280), BF)],
        2 * 512 * 512 * 1536,
    )(arrived.reshape(2, 64, 4, 2, 640), weights)
    right = lax.all_to_all(right, ("core",) + RAD + ("x",), 0, 0, tiled=True)
    solved = call(solve_kernel, bf16(512, 512), [VMEM] * 3, (), 2 * 512**3)(valid, solver, right)
    out = lax.all_to_all(solved.reshape(64, 8, 512), RAD, 0, 0, tiled=True)
    return out.transpose(1, 0, 2)


def solution(mesh):
    split = Mesh(mesh.devices.reshape(4, 2, 8, 8), LAT + RAD)
    placed = (
        P(RAD, LAT, None),
        P(RAD, None, LAT),
        P(),
        P(LAT + RAD, None, None),
        P(RAD, LAT, None),
    )
    return jax.shard_map(shards, mesh=split, in_specs=placed, out_specs=P(RAD, LAT, None), check_vma=False)
```

```python
import math

import jax
import jax.numpy as jnp
from jax import lax
from jax.experimental import pallas as pl
from jax.experimental.pallas import tpu as pltpu
from jax.sharding import Mesh, PartitionSpec as P

NR = 512
L = 512
LON = 1024
BF = jnp.bfloat16
F32 = jnp.float32
RAD = ("z", "y")
LAT = ("x", "core")


def nt_dot(a, b):
    return lax.dot_general(a, b, (((1,), (1,)), ((), ())), preferred_element_type=F32)


def iota(shape, dim):
    return lax.broadcasted_iota(jnp.int32, shape, dim)


def cos_sin(phase):
    quadrant = ((phase + 128) >> 8) & 3
    rest = ((phase + 128) & 255) - 128
    x = rest.astype(F32) * (2.0 * math.pi / LON)
    x2 = x * x
    sin_x = x * (1.0 + x2 * (-1.0 / 6 + x2 * (1.0 / 120 + x2 * (-1.0 / 5040 + x2 * (1.0 / 362880)))))
    cos_x = 1.0 + x2 * (-0.5 + x2 * (1.0 / 24 + x2 * (-1.0 / 720 + x2 * (1.0 / 40320))))
    swap = (quadrant & 1) == 1
    cos_part = jnp.where(swap, sin_x, cos_x)
    sin_part = jnp.where(swap, cos_x, sin_x)
    cos_sign = jnp.where((quadrant == 1) | (quadrant == 2), -1.0, 1.0)
    sin_sign = jnp.where(quadrant >= 2, -1.0, 1.0)
    return cos_part * cos_sign, sin_part * sin_sign


def fourier_kernel(
    assign_ref, forcing_hbm, previous_hbm, out_hbm, forcing_ref, previous_ref, table_ref, out_ref, in_sems, out_sems
):
    previous_copy = pltpu.make_async_copy(previous_hbm, previous_ref, in_sems.at[1])
    previous_copy.start()
    forcing_copy = pltpu.make_async_copy(forcing_hbm, forcing_ref, in_sems.at[0])
    forcing_copy.start()
    row = iota((512, 1), 0)
    slot = row >> 1
    orders = jnp.sum(jnp.where(iota((512, 256), 1) == slot, assign_ref[...], 0), axis=1, keepdims=True)
    lane = iota((512, 128), 1)
    cos_now, sin_now = cos_sin((orders * lane + (row & 1) * (LON // 4)) & (LON - 1))
    cos_half, sin_half = cos_now[:, 64:65], sin_now[:, 64:65]
    sign = (1 - 2 * (row & 1)).astype(F32)
    cos_step = jnp.broadcast_to(sign * (1.0 - 2.0 * sin_half * sin_half), (512, 128))
    sin_step = jnp.broadcast_to(sign * (2.0 * sin_half * cos_half), (512, 128))
    cos_now, sin_now = cos_now * LON**-0.5, sin_now * LON**-0.5
    for q in range(LON // 128):
        table_ref[:, q * 128 : q * 128 + 128] = cos_now.astype(BF)
        cos_now, sin_now = cos_now * cos_step - sin_now * sin_step, sin_now * cos_step + cos_now * sin_step
    previous_copy.wait()
    previous = previous_ref[...].reshape(512, 512).T
    forcing_copy.wait()
    out_copies = []
    for block in range(2):
        rows = slice(block * 256, block * 256 + 256)
        parts = []
        for h in range(3):
            part = forcing_ref[:, h * 32 : h * 32 + 32, :].reshape(256, LON)
            parts.append(nt_dot(table_ref[rows, :], part).astype(BF))
        before = previous[rows]
        for half in range(2):
            dests = pl.ds(half * 256 + block * 128, 128)
            pieces = [part[:, half * 128 : half * 128 + 128] for part in parts]
            pieces.append(before[:, half * 256 : half * 256 + 256])
            out_ref[dests] = jnp.concatenate(pieces, axis=1).reshape(128, 2, 640)
            sem = out_sems.at[block * 2 + half]
            copy = pltpu.make_async_copy(out_ref.at[dests], out_hbm.at[dests], sem)
            copy.start()
            out_copies.append(copy)
    for copy in out_copies:
        copy.wait()


def legendre_kernel(assign_ref, place_ref, legendre_ref, out_ref):
    order = jnp.sum(jnp.where(iota((1, 256), 1) == place_ref[0], assign_ref[...], 0), axis=1, keepdims=True)
    row = iota((512, 1), 0)
    core, x, inner = row >> 8, row & 3, (row >> 2) & 63
    degree = (2 * x + core) * 64 + inner
    column = iota((512, 512), 1)
    kept = jnp.where((column == degree) & (degree >= order), 1.0, 0.0).astype(BF)
    x_here = place_ref[2]
    for h in range(3):
        rows = pl.ds(h * 32, 32)
        for core_from in range(2):
            pieces = [legendre_ref[core_from, (x_here - x_from) & 3, rows, :] for x_from in range(4)]
            at = h * 256 + core_from * 128
            out_ref[:, at : at + 128] = nt_dot(kept, jnp.concatenate(pieces, axis=0)).astype(BF)
    out_ref[:, 768:1280] = jnp.where(column == core * 256 + x * 64 + inner, 2.0, 0.0).astype(BF)


def roll(a, shift):
    return pltpu.roll(a, shift, 1)


def spectrum_kernel(arrived_ref, weights_ref, out_ref, rows_ref, gathered_ref):
    for block in range(8):
        rows = slice(block * 128, block * 128 + 128)
        rows_ref[rows] = arrived_ref[block // 4, :, block % 4].reshape(128, 640)
    lane = iota((128, 128), 1)
    low_half = lane < 64
    even_quarter = (lane & 32) == 0

    def tile(block, at):
        return rows_ref[block * 128 : block * 128 + 128, at : at + 128].astype(F32)

    def place(rho, at, value):
        gathered_ref[rho * 128 : rho * 128 + 128, at : at + 128] = value.astype(BF)

    for h in range(3):
        for core in range(2):
            a = [tile(core * 4 + x, h * 128) for x in range(4)]
            b0 = jnp.where(low_half, a[0], roll(a[2], 64))
            b2 = jnp.where(low_half, roll(a[0], 64), a[2])
            b1 = jnp.where(low_half, a[1], roll(a[3], 64))
            b3 = jnp.where(low_half, roll(a[1], 64), a[3])
            at = h * 256 + core * 128
            place(0, at, jnp.where(even_quarter, b0, roll(b1, 32)))
            place(1, at, jnp.where(even_quarter, roll(b0, 96), b1))
            place(2, at, jnp.where(even_quarter, b2, roll(b3, 32)))
            place(3, at, jnp.where(even_quarter, roll(b2, 96), b3))
    for pair in range(2):
        for two in range(4):
            at = 384 + pair * 128
            a0, a1 = tile(two * 2, at), tile(two * 2 + 1, at)
            to = 768 + two * 128
            place(pair * 2, to, jnp.where(low_half, a0, roll(a1, 64)))
            place(pair * 2 + 1, to, jnp.where(low_half, roll(a0, 64), a1))
    right = nt_dot(weights_ref[...], gathered_ref[...]).astype(BF)
    row, column = iota((256, 1), 0), iota((256, 256), 1)
    parted = (column == (row & 1) * 128 + (row >> 1)).astype(BF)
    parts = []
    for i in range(2):
        part = right[:, i * 256 : i * 256 + 256]
        parts.append(jnp.dot(part, parted, preferred_element_type=F32).astype(BF))
    parts = [part[:, :128] for part in parts] + [part[:, 128:] for part in parts]
    out_ref[...] = jnp.concatenate(parts, axis=1).reshape(512, 2, 256)


def inverse_kernel(assign_ref, place_ref, inverse_ref, out_ref, valid_ref):
    inverse = inverse_ref[0].astype(BF)
    row, column = iota((256, 512), 0), iota((256, 512), 1)
    for half in range(2):
        radius = (row & 63) * 8 + half * 4 + (row >> 6)
        out_ref[half] = nt_dot(inverse, (column == radius).astype(BF)).astype(BF)
    valid = jnp.where(assign_ref[...] <= place_ref[1], 1.0, 0.0)
    doubled = (row == (column >> 1)).astype(BF)
    valid_ref[...] = jnp.dot(
        jnp.broadcast_to(valid, (8, 256)).astype(BF), doubled, preferred_element_type=F32
    )


def solve_kernel(valid_ref, inverse_ref, right_ref, out_ref):
    right = right_ref[...].reshape(1024, 256)
    solved = nt_dot(inverse_ref[0], right[:512]) + nt_dot(inverse_ref[1], right[512:])
    out_ref[...] = (solved * (valid_ref[0:1, :] * 0.5)).astype(BF)


VMEM = pl.BlockSpec(memory_space=pltpu.VMEM)
SMEM = pl.BlockSpec(memory_space=pltpu.SMEM)
HBM = pl.BlockSpec(memory_space=pltpu.HBM)


def call(kernel, out, ins, scratch=(), flops=0, vmem=16, outs=None):
    return pl.pallas_call(
        kernel,
        out_shape=out,
        in_specs=ins,
        out_specs=outs or jax.tree.map(lambda _: VMEM, out),
        scratch_shapes=list(scratch),
        compiler_params=pltpu.CompilerParams(vmem_limit_bytes=vmem * 1024 * 1024),
        cost_estimate=pl.CostEstimate(flops=flops, bytes_accessed=2 * 1024 * 1024, transcendentals=0),
    )


def bf16(*shape):
    return jax.ShapeDtypeStruct(shape, BF)


def shards(forcing, legendre, assign, inverse, previous):
    x, core, rad = lax.axis_index("x"), lax.axis_index("core"), lax.axis_index(RAD)
    orders = assign.reshape(1, 256)
    place = jnp.stack([rad * 4 + x, (x * 2 + core) * 64 + rad, x]).astype(jnp.int32)

    sent = call(
        fourier_kernel,
        bf16(512, 2, 640),
        [VMEM, HBM, HBM],
        [
            pltpu.VMEM((8, 96, LON), BF),
            pltpu.VMEM((8, 64, 512), BF),
            pltpu.VMEM((512, LON), BF),
            pltpu.VMEM((512, 2, 640), BF),
            pltpu.SemaphoreType.DMA((2,)),
            pltpu.SemaphoreType.DMA((4,)),
        ],
        2 * 512 * 768 * 1024,
        60,
        HBM,
    )(orders, forcing, previous)
    sent, legendre = lax.optimization_barrier((sent, legendre))
    arrived = lax.all_to_all(sent, ("core",) + RAD + ("x",), 0, 0, tiled=True)

    by_order = legendre.transpose(0, 2, 1)
    pieces = [lax.dynamic_index_in_dim(by_order, x, 0, keepdims=False)]
    for shift in range(1, 4):
        mine = lax.dynamic_index_in_dim(by_order, (x + shift) % 4, 0, keepdims=False)
        pieces.append(lax.ppermute(mine, "x", [(i, (i + shift) % 4) for i in range(4)]))
    whole = lax.all_gather(jnp.stack(pieces), "core", axis=0)
    weights = call(legendre_kernel, bf16(512, 1280), [VMEM, SMEM, VMEM], (), 2 * 512 * 512 * 768)(
        orders, place, whole
    )
    solver, valid = call(
        inverse_kernel,
        (bf16(2, 512, 256), jax.ShapeDtypeStruct((8, 512), F32)),
        [VMEM, SMEM, VMEM],
        (),
        2 * 512**3,
    )(orders, place, inverse)

    weights, solver, valid = lax.optimization_barrier((weights, solver, valid))
    right = call(
        spectrum_kernel,
        bf16(512, 2, 256),
        [VMEM] * 2,
        [pltpu.VMEM((1024, 640), BF), pltpu.VMEM((512, 1280), BF)],
        2 * 512 * 512 * 1536,
    )(arrived.reshape(2, 64, 4, 2, 640), weights)
    right = lax.all_to_all(right, ("core",) + RAD + ("x",), 0, 0, tiled=True)
    solved = call(solve_kernel, bf16(512, 512), [VMEM] * 3, (), 2 * 512**3)(valid, solver, right)
    out = lax.all_to_all(solved.reshape(64, 8, 512), RAD, 0, 0, tiled=True)
    return out.transpose(1, 0, 2)


def solution(mesh):
    split = Mesh(mesh.devices.reshape(4, 2, 8, 8), LAT + RAD)
    placed = (
        P(RAD, LAT, None),
        P(RAD, None, LAT),
        P(),
        P(LAT + RAD, None, None),
        P(RAD, LAT, None),
    )
    return jax.shard_map(shards, mesh=split, in_specs=placed, out_specs=P(RAD, LAT, None), check_vma=False)
```
